512 devices in a mesh: tile: 128 (over y, z, core), mem: 4 (over x).
Axes of the slice: x: 4, y: 8, z: 8, core: 2. Of those that a mesh axis runs over, the one named last changes fastest.
Arguments:
- background: bfloat16 [1792, 80, 512], P('tile', 'mem'), may hold values from -6 to 6
- obs_ens: bfloat16 [1792, 80, 128], P('tile', 'mem'), may hold values from -6 to 6
- innovation: float32 [1792, 128], P('tile'), may hold values from -6 to 6
- precision: float32 [1792, 128], P('tile'), may hold values from 0.1 to 2
- loc_weight: float32 [1792, 7], P('tile'), may hold values from 0.1 to 1
- old_split: int32 [129], replicated, may hold values from 0 to 1024, as said below
- new_split: int32 [129], replicated, may hold values from 0 to 1024, as said below
- obs_count: int32 [1792], P('tile'), may hold values from 32 to 128
- halo_tiles: int32 [128, 12], replicated, may hold values from 0 to 1023, as said below
- region_list: int32 [1792, 7], P('tile'), may hold values from 0 to 25, as said below
Outputs:
- analysis: bfloat16 [1792, 80, 512], P('tile', 'mem')
The draws below stay inside these ranges and needn't reach their ends.
Inputs may be any that keep to these rules, and one draw needn't show every extreme that they name: old_split[0] = 0 and old_split[128] = 1024; each device holds between 2 and 14 old tiles, exactly 14 on some device. new_split[0] = 0 and new_split[128] = 1024; each device holds between 6 and 10 new tiles; every new_split[d] differs from old_split[d] by at most 2, by exactly 2 for some d. `halo_tiles`: row d is 3 groups of 4 entries; a group holds distinct tiles in rising order that one device p other than d holds under new_split, with p within 3 of d, and the 3 devices of a row are distinct. `region_list`: for a slot of device d, an entry r < 14 names d's slot r, which is live; an entry r >= 14 names the tile halo_tiles[d, r - 14].
All inputs are finite; a program needn't handle non-finite values.
Results may differ from the reference program's by a relative error of at most 0.0057.
Values may be sent and summed in bfloat16 or wider, within the bound.
No kernel may reach another device: no remote copies, remote signals or barrier semaphores. Data moves between devices by JAX's collectives and lax.ppermute only.
A program may use at most 64 MiB of HBM per device.

```python
import math
import jax
import jax.numpy as jnp
from jax import lax

MEMBERS = 80
STATE = 512
OBS_T = 128
TILE_MEAN = 8
CAP = 14
JITTER = 3
MOVE = 2
TILES = 1024
SLOTS = 1792
REACH = 3
HPEER = 3
HCAP = 4
HLIST = 12
NBR = 7
NS_ITERS = 6
N_TILE = 128


def split_pair(key):
    inner_key = jax.random.fold_in(key, 11)
    jitter_key, widest_key = jax.random.split(inner_key)
    boundary = jnp.arange(N_TILE + 1, dtype=jnp.int32)
    jitter = jax.random.randint(jitter_key, (N_TILE + 1,), -JITTER, JITTER + 1)
    widest = jax.random.randint(widest_key, (), 1, N_TILE - 1)
    jitter = jnp.where(boundary == widest, -JITTER, jitter)
    jitter = jnp.where(boundary == widest + 1, JITTER, jitter)
    jitter = jnp.where((boundary == 0) | (boundary == N_TILE), 0, jitter)
    old_bounds = boundary * TILE_MEAN + jitter
    moved_by = jnp.clip(jitter, -MOVE, MOVE)
    new_bounds = old_bounds - moved_by
    return (old_bounds.astype(jnp.int32), new_bounds.astype(jnp.int32))


def draw_old_split(key, part):
    return split_pair(key)[0]


def draw_new_split(key, part):
    return split_pair(key)[1]


def draw_halo_tiles(key, part):
    old_bounds, new_bounds = split_pair(key)
    inner_key = jax.random.fold_in(key, 23)
    peer_key, slot_key = jax.random.split(inner_key)
    offsets = jnp.concatenate([jnp.arange(-REACH, 0), jnp.arange(1, REACH + 1)]).astype(jnp.int32)
    device = jnp.arange(N_TILE, dtype=jnp.int32)
    target = device[:, None] + offsets[None, :]
    inside = (target >= 0) & (target < N_TILE)
    scores = jax.random.randint(peer_key, (N_TILE, 2 * REACH), 0, 1 << 20) * (2 * REACH) + jnp.arange(2 * REACH)[None, :]
    scores = jnp.where(inside, scores, (1 << 30) + jnp.arange(2 * REACH)[None, :])
    ranking = jnp.argsort(scores, axis=1, stable=True)[:, :HPEER]
    peer_ids = jnp.take_along_axis(target, ranking, axis=1)
    counts = new_bounds[1:] - new_bounds[:-1]
    peer_count = counts[peer_ids]
    slot_scores = jax.random.randint(slot_key, (N_TILE, HPEER, CAP), 0, 1 << 20) * CAP + jnp.arange(CAP)[None, None, :]
    slot_scores = jnp.where(jnp.arange(CAP)[None, None, :] < peer_count[:, :, None], slot_scores, (1 << 30) + jnp.arange(CAP)[None, None, :])
    chosen = jnp.sort(jnp.argsort(slot_scores, axis=2, stable=True)[:, :, :HCAP], axis=2)
    positions = new_bounds[peer_ids][:, :, None] + chosen
    return positions.reshape(N_TILE, HLIST).astype(jnp.int32)


def draw_region_list(key, part):
    old_bounds, new_bounds = split_pair(key)
    inner_key = jax.random.fold_in(key, 37)
    kind_key, own_key, far_key = jax.random.split(inner_key, 3)
    counts = new_bounds[1:] - new_bounds[:-1]
    count_per_slot = jnp.repeat(counts, CAP, total_repeat_length=N_TILE * CAP)
    own_pick = jax.random.randint(own_key, (N_TILE * CAP, NBR), 0, 1 << 20) % count_per_slot[:, None]
    far_pick = CAP + jax.random.randint(far_key, (N_TILE * CAP, NBR), 0, HLIST)
    choose_far = jax.random.randint(kind_key, (N_TILE * CAP, NBR), 0, 2)
    return jnp.where(choose_far == 1, far_pick, own_pick).astype(jnp.int32)


def place_ends(array, rng, low, high):
    longest = array.shape.index(max(array.shape))
    spots = []
    for shift in (0, 1):
        where = [jax.random.randint(jax.random.fold_in(rng, axis), (), 0, length) for axis, length in enumerate(array.shape)]
        where[longest] = (where[longest] + shift) % array.shape[longest]
        spots.append(tuple(where))
    return array.at[spots[0]].set(low).at[spots[1]].set(high)


def block_scale(rng, dims, pieces, least, high):
    loudness = 1.0
    for dim, parts in pieces:
        steps = jax.random.uniform(jax.random.fold_in(jax.random.fold_in(rng, 6), dim), (parts,), jnp.float32, least / len(pieces), high / len(pieces))
        loudness = loudness * jnp.repeat(jnp.exp(steps), dims[dim] // parts).reshape((-1,) + (1,) * (len(dims) - 1 - dim))
    return loudness


def noise(key, extent, scale, reach, cuts=(), held_as=jnp.bfloat16):
    level = block_scale(key, extent, cuts, -0.22, 0.18) if cuts else 1.0
    values = jax.random.normal(key, extent, jnp.float32) * scale * level
    return jnp.minimum(jnp.maximum(values, -reach), reach).astype(held_as)


def setup_inputs(seed: int = 0) -> dict:
    arg_keys = jax.random.split(jax.random.key(seed), 11)
    background = noise(arg_keys[0], (SLOTS, MEMBERS, STATE), 1.0, 6.0, ((0, 128), (1, 4)))
    obs_ens = noise(arg_keys[1], (SLOTS, MEMBERS, OBS_T), 1.0, 6.0, ((0, 128), (1, 4)))
    innovation = noise(arg_keys[2], (SLOTS, OBS_T), 1.0, 6.0, ((0, 128),), jnp.float32)
    precision = jnp.clip(jnp.exp(math.log(2.0) - 2.9957323 * jax.random.uniform(arg_keys[3], (SLOTS, OBS_T), jnp.float32) ** block_scale(arg_keys[3], (SLOTS, OBS_T), ((0, 128),), -0.2, 0.2)), 0.1, 2.0)
    loc_weight = jnp.clip(jnp.exp(math.log(1.0) - 2.3025851 * jax.random.uniform(arg_keys[4], (SLOTS, NBR), jnp.float32) ** block_scale(arg_keys[4], (SLOTS, NBR), ((0, 128),), -0.2, 0.2)), 0.1, 1.0)
    old_split = draw_old_split(jax.random.fold_in(arg_keys[10], 71), 0)
    new_split = draw_new_split(jax.random.fold_in(arg_keys[10], 71), 0)
    obs_count = place_ends(jax.random.randint(arg_keys[7], (SLOTS,), OBS_T // 4, OBS_T + 1), jax.random.fold_in(arg_keys[7], 1), OBS_T // 4, OBS_T).astype(jnp.int32)
    halo_tiles = draw_halo_tiles(jax.random.fold_in(arg_keys[10], 71), 0)
    region_list = draw_region_list(jax.random.fold_in(arg_keys[10], 71), 0)
    return dict(background=background, obs_ens=obs_ens, innovation=innovation, precision=precision, loc_weight=loc_weight, old_split=old_split, new_split=new_split, obs_count=obs_count, halo_tiles=halo_tiles, region_list=region_list)


inflation = 1.1
exact = lax.Precision.HIGHEST

def owner_of(split_points, position):
    bounds = split_points[1:]
    return lax.optimization_barrier(jnp.sum((bounds[None, :] <= position[:, None]).astype(jnp.int32), axis=1)).astype(jnp.int32)

def inverse_root(system, repeats):
    identity = jnp.eye(system.shape[-1], dtype=system.dtype)
    frobenius = jnp.sqrt(lax.optimization_barrier(jnp.sum(system * system, axis=(1, 2))))
    root_part = system / frobenius[:, None, None]
    inverse_part = jnp.broadcast_to(identity, system.shape)
    for repeat in range(repeats):
        middle = 0.5 * (3.0 * identity - jnp.einsum('pij,pjk->pik', inverse_part, root_part, precision=exact))
        root_part = jnp.einsum('pij,pjk->pik', root_part, middle, precision=exact)
        inverse_part = jnp.einsum('pij,pjk->pik', middle, inverse_part, precision=exact)
    return (inverse_part, frobenius)

def reference(background, obs_ens, innovation, precision, loc_weight, old_split, new_split, obs_count, halo_tiles, region_list):
    slot_all = jnp.arange(N_TILE * CAP, dtype=jnp.int32)
    device = (slot_all // CAP).astype(jnp.int32)
    within = (slot_all % CAP).astype(jnp.int32)
    tile_pos = new_split[device] + within
    live_slot = tile_pos < new_split[device + 1]
    safe_pos = jnp.minimum(tile_pos, TILES - 1).astype(jnp.int32)
    old_owner = owner_of(old_split, safe_pos)
    old_slot = (old_owner * CAP + safe_pos - old_split[old_owner]).astype(jnp.int32)
    live_obs = (jnp.arange(OBS_T, dtype=jnp.int32)[None, :] < obs_count[:, None]).astype(jnp.float32)
    root_weight = jnp.sqrt(precision * live_obs)
    scaled = (obs_ens.astype(jnp.float32) * root_weight[:, None, :]).astype(jnp.bfloat16)
    pulled = (root_weight * innovation).astype(jnp.bfloat16)
    flat_halo = halo_tiles.reshape(-1)
    halo_owner = owner_of(new_split, flat_halo)
    halo_slot = (halo_owner * CAP + flat_halo - new_split[halo_owner]).astype(jnp.int32).reshape(N_TILE, HLIST)
    own_slot = device[:, None] * CAP + region_list
    far_slot = halo_slot[device[:, None], jnp.clip(region_list - CAP, 0, HLIST - 1)]
    entry_slot = jnp.where(region_list < CAP, own_slot, far_slot).astype(jnp.int32)
    entry_slot = jnp.concatenate([slot_all[:, None], entry_slot], axis=1)
    entry_weight = jnp.concatenate([jnp.ones((N_TILE * CAP, 1), jnp.float32), loc_weight], axis=1)

    def one_device(device_index):
        slot_ids = (device_index * CAP + jnp.arange(CAP, dtype=jnp.int32)).astype(jnp.int32)
        region_rows = entry_slot[slot_ids]
        row_weights = entry_weight[slot_ids]
        region = scaled[region_rows].astype(jnp.float32)
        region_pulled = pulled[region_rows].astype(jnp.float32)
        products = jnp.einsum('pekn,pejn->pekj', region, region, precision=exact)
        gram_matrix = lax.optimization_barrier(jnp.sum(row_weights[:, :, None, None] * products, axis=1))
        pull_terms = jnp.einsum('pekn,pen->pek', region, region_pulled, precision=exact)
        pull_sum = lax.optimization_barrier(jnp.sum(row_weights[:, :, None] * pull_terms, axis=1))
        identity = jnp.eye(MEMBERS, dtype=jnp.float32)
        system = gram_matrix + (MEMBERS - 1) / inflation * identity
        inverse, frobenius = inverse_root(system, NS_ITERS)
        spread = (math.sqrt(MEMBERS - 1) / jnp.sqrt(frobenius))[:, None, None] * inverse
        half_way = jnp.einsum('pij,pj->pi', inverse, pull_sum, precision=exact)
        mean_weight = jnp.einsum('pij,pj->pi', inverse, half_way, precision=exact) / frobenius[:, None]
        transform = (spread + mean_weight[:, :, None]).astype(jnp.bfloat16).astype(jnp.float32)
        state_rows = background[old_slot[slot_ids]].astype(jnp.float32)
        mean_state = lax.optimization_barrier(jnp.sum(state_rows, axis=1)) / MEMBERS
        keep_share = 1.0 - lax.optimization_barrier(jnp.sum(transform, axis=1))
        analysis_rows = jnp.einsum('pij,pis->pjs', transform, state_rows, precision=exact) + keep_share[:, :, None] * mean_state[:, None, :]
        return jnp.where(live_slot[slot_ids][:, None, None], analysis_rows, 0.0).astype(jnp.bfloat16)
    result = lax.map(one_device, jnp.arange(N_TILE, dtype=jnp.int32))
    return result.reshape(N_TILE * CAP, MEMBERS, STATE)
```

```python
import functools
import math

import jax
import jax.numpy as jnp
from jax import lax
from jax.experimental import pallas as pl
from jax.experimental.pallas import tpu as pltpu
from jax.sharding import PartitionSpec as P

MOVE = 2
REACH = 3
HPEER = 3
HCAP = 4
NS_ITERS = 6
LIVE = 10
BLOCK = 4
PADDED = 24
INFLATION = 1.1

SWAPS = ((-3, 3, -3, 3), (-2, -2, 2, 2), (-1, -3, 3, 1))

SMEM = pltpu.SMEM
VMEM = pltpu.VMEM
F32 = jnp.float32
BF16 = jnp.bfloat16


def chosen(place, values):
    result = values[0]
    for k in range(1, len(values)):
        result = jnp.where(place == k, values[k], result)
    return result


def padded_rows(x, extra=()):
    rows = x.shape[0] + len(extra)
    zeros = jnp.zeros((PADDED - rows, x.shape[1]), x.dtype)
    return jnp.concatenate([x, *extra, zeros], axis=0)


def pack_kernel(
    count_ref, old_ref, new_ref, halo_ref,
    obs_ref, innovation_ref, precision_ref, background_ref,
    own_ref, block_ref, *swap_refs,
):
    devices = new_ref.shape[0] - 1
    me = lax.axis_index("tile")
    place = lax.rem(me, BLOCK)
    new_start, new_end = new_ref[me], new_ref[me + 1]
    members, obs_slots = obs_ref.shape[1:]
    lane = lax.broadcasted_iota(jnp.int32, (1, obs_slots), 1)
    for i in range(LIVE):
        live = (lane < count_ref[i]).astype(F32)
        root = jnp.sqrt(precision_ref[i : i + 1, :] * live)
        scaled = obs_ref[i].astype(F32) * root
        pulled = root * innovation_ref[i : i + 1, :]
        own_ref[i] = padded_rows(scaled, (pulled,)).astype(BF16)

    def pack(reader, put):
        reader = jnp.clip(reader, 0, devices - 1)
        group = 0
        for g in range(1, HPEER):
            first = halo_ref[reader, g * HCAP]
            group = jnp.where((first >= new_start) & (first < new_end), g, group)
        for k in range(HCAP):
            row = jnp.clip(halo_ref[reader, group * HCAP + k] - new_start, 0, LIVE - 1)
            put(k, own_ref[row])

    for j in range(BLOCK):
        def put(k, value, j=j):
            block_ref[j, k] = value
        pack(me - place + j, put)
    for swap, swap_ref in zip(SWAPS, swap_refs):
        def put(k, value, swap_ref=swap_ref):
            swap_ref[k] = value
        pack(me + chosen(place, swap), put)

    old_count = old_ref[me + 1] - old_ref[me]
    pieces = background_ref.shape[2] // obs_slots
    for first, inside, slot in (
        (old_count - MOVE, place < BLOCK - 1, place + 1),
        (0, place > 0, place - 1),
    ):
        for t in range(MOVE):
            value = padded_rows(background_ref[first + t].astype(F32)).astype(BF16)
            for c in range(pieces):
                piece = value[:, c * obs_slots : (c + 1) * obs_slots]
                at = HCAP + t * pieces + c

                @pl.when(inside)
                def _():
                    block_ref[slot, at] = piece

                @pl.when(jnp.logical_not(inside))
                def _():
                    swap_refs[-1][at] = piece


def table_kernel(new_ref, halo_ref, own_ref, block_ref, *refs):
    swap_refs, out_ref = refs[:-1], refs[-1]
    devices = new_ref.shape[0] - 1
    me = lax.axis_index("tile")
    place = lax.rem(me, BLOCK)
    copies = out_ref.shape[0]
    moved = block_ref.shape[1] - HCAP

    def put(at, value):
        for r in range(copies):
            out_ref[r, at] = value

    for i in range(LIVE):
        put(i, own_ref[i])
    for g in range(HPEER):
        first = halo_ref[me, g * HCAP]
        peer = me - REACH
        for o in range(1 - REACH, REACH + 1):
            bound = new_ref[jnp.clip(me + o, 0, devices)]
            peer = peer + (bound <= first).astype(jnp.int32)
        at = LIVE + g * HCAP
        base = me - place

        @pl.when((peer >= base) & (peer < base + BLOCK))
        def _():
            slot = jnp.clip(peer - base, 0, BLOCK - 1)
            for k in range(HCAP):
                put(at + k, block_ref[slot, k])

        for swap, swap_ref in zip(SWAPS, swap_refs):
            @pl.when(peer == me + chosen(place, swap))
            def _():
                for k in range(HCAP):
                    put(at + k, swap_ref[k])

    for at, inside, slot in (
        (LIVE + HPEER * HCAP, place > 0, place - 1),
        (LIVE + HPEER * HCAP + moved, place < BLOCK - 1, place + 1),
    ):
        @pl.when(inside)
        def _():
            for k in range(moved):
                put(at + k, block_ref[slot, HCAP + k])

        @pl.when(jnp.logical_not(inside))
        def _():
            for k in range(moved):
                put(at + k, swap_refs[-1][HCAP + k])


def split(x):
    high = x.astype(BF16)
    return high, (x - high.astype(F32)).astype(BF16)


def dot(a, b):
    return jnp.dot(a, b, preferred_element_type=F32)


def dot3(a, b):
    return dot(a[0], b[0]) + (dot(a[0], b[1]) + dot(a[1], b[0]))


def analysis_kernel(
    region_ref, weight_ref, old_ref, new_ref,
    table_ref, background_ref, out_ref,
    gram_ref, system_ref, inverse_ref, state_ref,
):
    me = lax.axis_index("tile")
    rank = lax.axis_index("mem")
    ranks, tiles = table_ref.shape[0], LIVE + HPEER * HCAP
    capacity, members, width = out_ref.shape
    obs_slots = table_ref.shape[3]
    side = ranks * PADDED
    ensemble = ranks * members
    old_start, old_end = old_ref[me], old_ref[me + 1]
    new_start, new_end = new_ref[me], new_ref[me + 1]

    row = lax.broadcasted_iota(jnp.int32, (side, side), 0)
    column = lax.broadcasted_iota(jnp.int32, (side, side), 1)
    real = (lax.rem(row, PADDED) < members) & (lax.rem(column, PADDED) < members)
    diagonal = (row == column).astype(F32)
    shift = jnp.where(real, diagonal * ((ensemble - 1) / INFLATION), 0.0)
    lane = lax.broadcasted_iota(jnp.int32, (1, side), 1)
    real_lane = lax.rem(lane, PADDED) < members

    for t in range(tiles):
        rows = [table_ref[r, t].astype(F32) for r in range(ranks)]
        block = jnp.concatenate(rows, axis=0).astype(BF16)
        gram_ref[t] = lax.dot_general(
            block, block, (((1,), (1,)), ((), ())), preferred_element_type=F32
        )

    pieces = width // obs_slots
    for i in range(LIVE):
        tile = new_start + i
        stays = (tile >= old_start) & (tile < old_end)

        @pl.when(stays)
        def _():
            at = jnp.clip(tile - old_start, 0, capacity - 1)
            rows = [padded_rows(background_ref[r * capacity + at].astype(F32)) for r in range(ranks)]
            state_ref[i] = jnp.concatenate(rows, axis=0).astype(BF16)

        @pl.when(jnp.logical_not(stays))
        def _():
            left = jnp.clip(tile - old_start + MOVE, 0, MOVE - 1) * pieces
            right = (jnp.clip(tile - old_end, 0, MOVE - 1) + MOVE) * pieces
            at = tiles + jnp.where(tile < old_start, left, right)
            for c in range(pieces):
                rows = [table_ref[r, at + c].astype(F32) for r in range(ranks)]
                state_ref[i, :, c * obs_slots : (c + 1) * obs_slots] = jnp.concatenate(
                    rows, axis=0
                ).astype(BF16)

    frobenius, pull = [], []
    for i in range(LIVE):
        total = gram_ref[i]
        for e in range(region_ref.shape[1]):
            r = region_ref[i, e]
            at = jnp.where(r < capacity, jnp.minimum(r, LIVE - 1), r - capacity + LIVE)
            total = total + weight_ref[i, e] * gram_ref[at]
        pull.append(jnp.where(real_lane, total[members : members + 1, :], 0.0))
        system = jnp.where(real, total, 0.0) + shift
        squared = jnp.sum(jnp.sum(system * system, axis=0, keepdims=True), axis=1, keepdims=True)
        norm = jnp.sqrt(squared)
        frobenius.append(norm)
        root = system * (1.0 / norm)
        middle = 1.5 * diagonal - 0.5 * root
        inverse_ref[i] = middle
        system_ref[i] = dot3(split(root), split(middle))

    for step in range(1, NS_ITERS):
        for i in range(LIVE):
            root, inverse = split(system_ref[i]), split(inverse_ref[i])
            middle = split(1.5 * diagonal - 0.5 * dot3(inverse, root))
            if step < NS_ITERS - 1:
                system_ref[i] = dot3(root, middle)
            inverse_ref[i] = dot3(middle, inverse)

    own_row = lax.broadcasted_iota(jnp.int32, (PADDED, side), 0)
    for i in range(LIVE):
        inverse = split(inverse_ref[i])
        pulled = jnp.broadcast_to(pull[i], (8, side))
        half_way = dot3(split(pulled), inverse)
        mean_weight = dot3(split(half_way), inverse)[0:1, :] / frobenius[i]
        own = inverse_ref[i, pl.ds(pl.multiple_of(rank * PADDED, 8), PADDED), :]
        spread = (math.sqrt(ensemble - 1) / jnp.sqrt(frobenius[i])) * own
        transform = jnp.where((own_row < members) & real_lane, spread + mean_weight, 0.0)
        transform = transform.astype(BF16)
        keep_share = 1.0 - jnp.sum(transform.astype(F32), axis=1, keepdims=True)
        ones = jnp.where((own_row == members) & real_lane, 1.0, 0.0).astype(BF16)
        blended = dot(transform + ones, state_ref[i])
        mean_state = blended[members : members + 1, :] / ensemble
        analysis = blended[:members] + keep_share[:members] * mean_state
        out_ref[i] = jnp.where(new_start + i < new_end, analysis, 0.0).astype(BF16)
    for i in range(LIVE, capacity):
        out_ref[i] = jnp.zeros((members, width), BF16)


def shards(
    background, obs_ens, innovation, precision, loc_weight,
    old_split, new_split, obs_count, halo_tiles, region_list,
):
    capacity, members, width = background.shape
    obs_slots = obs_ens.shape[2]
    devices = lax.axis_size("tile")
    ranks = lax.axis_size("mem")
    moved = MOVE * width // obs_slots
    tiles = LIVE + HPEER * HCAP
    smem = pl.BlockSpec(memory_space=SMEM)
    vmem = pl.BlockSpec(memory_space=VMEM)

    def tile_blocks(*leading):
        return jax.ShapeDtypeStruct((*leading, PADDED, obs_slots), BF16)

    gathered = lax.all_gather(background, "mem", axis=0, tiled=True)

    own, block, *swaps = pl.pallas_call(
        pack_kernel,
        out_shape=(
            tile_blocks(LIVE),
            tile_blocks(BLOCK, HCAP + moved),
            tile_blocks(HCAP),
            tile_blocks(HCAP),
            tile_blocks(HCAP + moved),
        ),
        in_specs=[smem] * 4 + [vmem] * 4,
        out_specs=[vmem] * 5,
        compiler_params=pltpu.CompilerParams(vmem_limit_bytes=16 << 20),
    )(obs_count, old_split, new_split, halo_tiles, obs_ens, innovation, precision, background)

    groups = [list(range(b, b + BLOCK)) for b in range(0, devices, BLOCK)]
    block = lax.all_to_all(block, "tile", 0, 0, axis_index_groups=groups, tiled=True)
    arrived = []
    for swap, value in zip(SWAPS, swaps):
        pairs = [(d, d + swap[d % BLOCK]) for d in range(devices)]
        pairs = [(d, e) for d, e in pairs if 0 <= e < devices]
        arrived.append(lax.ppermute(value, "tile", pairs))

    table = pl.pallas_call(
        table_kernel,
        out_shape=tile_blocks(ranks, tiles + 2 * moved),
        in_specs=[smem] * 2 + [vmem] * 5,
        out_specs=vmem,
        compiler_params=pltpu.CompilerParams(vmem_limit_bytes=16 << 20),
    )(new_split, halo_tiles, own, block, *arrived)
    table = lax.all_to_all(table, "mem", 0, 0, tiled=True)

    side = ranks * PADDED
    return pl.pallas_call(
        analysis_kernel,
        out_shape=jax.ShapeDtypeStruct((capacity, members, width), BF16),
        in_specs=[smem] * 4 + [vmem] * 2,
        out_specs=vmem,
        scratch_shapes=[
            VMEM((tiles, side, side), F32),
            VMEM((LIVE, side, side), F32),
            VMEM((LIVE, side, side), F32),
            VMEM((LIVE, side, width), BF16),
        ],
        compiler_params=pltpu.CompilerParams(vmem_limit_bytes=28 << 20),
    )(region_list, loc_weight, old_split, new_split, table, gathered)


def solution(mesh):
    in_specs = (
        P("tile", "mem", None),
        P("tile", "mem", None),
        P("tile", None),
        P("tile", None),
        P("tile", None),
        P(),
        P(),
        P("tile"),
        P(),
        P("tile", None),
    )
    out_specs = P("tile", "mem", None)
    return jax.shard_map(shards, mesh=mesh, in_specs=in_specs, out_specs=out_specs, check_vma=False)
```

```python
import functools
import math

import jax
import jax.numpy as jnp
from jax import lax
from jax.experimental import pallas as pl
from jax.experimental.pallas import tpu as pltpu
from jax.sharding import PartitionSpec as P

MOVE = 2
REACH = 3
HPEER = 3
HCAP = 4
NS_ITERS = 6
LIVE = 10
BLOCK = 4
PADDED = 24
INFLATION = 1.1
PITCH = 16

SWAPS = ((-3, 3, -3, 3), (-2, -2, 2, 2), (-1, -3, 3, 1))

SMEM = pltpu.SMEM
VMEM = pltpu.VMEM
F32 = jnp.float32
BF16 = jnp.bfloat16


def chosen(place, values):
    result = values[0]
    for k in range(1, len(values)):
        result = jnp.where(place == k, values[k], result)
    return result


def padded_rows(x, extra=()):
    rows = x.shape[0] + len(extra)
    zeros = jnp.zeros((PADDED - rows, x.shape[1]), x.dtype)
    return jnp.concatenate([x, *extra, zeros], axis=0)


def pack_kernel(
    count_ref, old_ref, new_ref, halo_ref,
    obs_ref, innovation_ref, precision_ref, background_ref,
    own_ref, state_ref, block_ref, *refs,
):
    swap_refs, (obs_rows, state_rows) = refs[:-2], refs[-2:]
    devices = new_ref.shape[0] - 1
    me = lax.axis_index("tile")
    place = lax.rem(me, BLOCK)
    new_start, new_end = new_ref[me], new_ref[me + 1]
    members, capacity, obs_slots = obs_ref.shape
    pieces = background_ref.shape[2] // obs_slots

    lane = lax.broadcasted_iota(jnp.int32, (1, obs_slots), 1)
    live = [(lane < count_ref[i]).astype(F32) for i in range(capacity)]
    root = jnp.sqrt(precision_ref[...] * jnp.concatenate(live, axis=0))
    pulled = root * innovation_ref[...]
    for m in range(members):
        obs_rows[m * PITCH : m * PITCH + capacity, :] = obs_ref[m].astype(F32) * root
        for c in range(pieces):
            span = slice(c * obs_slots, (c + 1) * obs_slots)
            state_rows[c, m * PITCH : m * PITCH + capacity, :] = background_ref[m, :, span].astype(F32)
    for i in range(LIVE):
        scaled = obs_rows[pl.ds(i, members, stride=PITCH), :]
        own_ref[i] = padded_rows(scaled, (pulled[i : i + 1, :],)).astype(BF16)
    for i in range(capacity):
        for c in range(pieces):
            rows = state_rows[c, pl.ds(i, members, stride=PITCH), :]
            state_ref[i, c] = padded_rows(rows).astype(BF16)

    def pack(reader, put):
        reader = jnp.clip(reader, 0, devices - 1)
        group = 0
        for g in range(1, HPEER):
            first = halo_ref[g * HCAP, reader]
            group = jnp.where((first >= new_start) & (first < new_end), g, group)
        for k in range(HCAP):
            row = jnp.clip(halo_ref[group * HCAP + k, reader] - new_start, 0, LIVE - 1)
            put(k, own_ref[row])

    for j in range(BLOCK):
        def put(k, value, j=j):
            block_ref[j, k] = value
        pack(me - place + j, put)
    for swap, swap_ref in zip(SWAPS, swap_refs):
        def put(k, value, swap_ref=swap_ref):
            swap_ref[k] = value
        pack(me + chosen(place, swap), put)

    old_count = old_ref[me + 1] - old_ref[me]
    for first, inside, slot in (
        (old_count - MOVE, place < BLOCK - 1, place + 1),
        (0, place > 0, place - 1),
    ):
        for t in range(MOVE):
            for c in range(pieces):
                piece = state_ref[first + t, c]
                at = HCAP + t * pieces + c

                @pl.when(inside)
                def _():
                    block_ref[slot, at] = piece

                @pl.when(jnp.logical_not(inside))
                def _():
                    swap_refs[-1][at] = piece


def table_kernel(
    old_hbm, new_hbm, halo_hbm, own_hbm, state_hbm, block_ref, *refs
):
    swap_refs, (out_ref, table_ref, state_ref, old_ref, new_ref, halo_ref, sems) = refs[:-7], refs[-7:]
    fetches = [
        pltpu.make_async_copy(source, target, sems.at[k])
        for k, (source, target) in enumerate((
            (old_hbm, old_ref),
            (new_hbm, new_ref),
            (halo_hbm, halo_ref),
            (own_hbm, table_ref.at[pl.ds(0, LIVE)]),
            (state_hbm, state_ref),
        ))
    ]
    for fetch in fetches:
        fetch.start()
    for fetch in fetches:
        fetch.wait()
    devices = new_ref.shape[0] - 1
    me = lax.axis_index("tile")
    place = lax.rem(me, BLOCK)
    base = me - place
    old_start, old_end, new_start = old_ref[me], old_ref[me + 1], new_ref[me]
    pieces = state_ref.shape[1]

    for g in range(HPEER):
        first = halo_ref[g * HCAP, me]
        peer = me - REACH
        for o in range(1 - REACH, REACH + 1):
            bound = new_ref[jnp.clip(me + o, 0, devices)]
            peer = peer + (bound <= first).astype(jnp.int32)
        at = LIVE + g * HCAP

        @pl.when((peer >= base) & (peer < base + BLOCK))
        def _():
            slot = jnp.clip(peer - base, 0, BLOCK - 1)
            for k in range(HCAP):
                table_ref[at + k] = block_ref[slot, k]

        for swap, swap_ref in zip(SWAPS, swap_refs):
            @pl.when(peer == me + chosen(place, swap))
            def _():
                for k in range(HCAP):
                    table_ref[at + k] = swap_ref[k]

    for i in range(LIVE):
        tile = new_start + i
        at = LIVE + HPEER * HCAP + i * pieces
        stays = (tile >= old_start) & (tile < old_end)
        from_left = tile < old_start
        inside = jnp.where(from_left, place > 0, place < BLOCK - 1)
        left = jnp.clip(tile - old_start + MOVE, 0, MOVE - 1)
        right = jnp.clip(tile - old_end, 0, MOVE - 1)
        begin = HCAP + jnp.where(from_left, left, right) * pieces
        slot = jnp.clip(jnp.where(from_left, place - 1, place + 1), 0, BLOCK - 1)

        @pl.when(stays)
        def _():
            own = jnp.clip(tile - old_start, 0, state_ref.shape[0] - 1)
            for c in range(pieces):
                table_ref[at + c] = state_ref[own, c]

        @pl.when(jnp.logical_not(stays) & inside)
        def _():
            for c in range(pieces):
                table_ref[at + c] = block_ref[slot, begin + c]

        @pl.when(jnp.logical_not(stays) & jnp.logical_not(inside))
        def _():
            for c in range(pieces):
                table_ref[at + c] = swap_refs[-1][begin + c]

    copies = [
        pltpu.make_async_copy(table_ref, out_ref.at[r], sems.at[r])
        for r in range(out_ref.shape[0])
    ]
    for copy in copies:
        copy.start()
    for copy in copies:
        copy.wait()


def split(x):
    high = x.astype(BF16)
    return high, (x - high.astype(F32)).astype(BF16)


def dot(a, b):
    return jnp.dot(a, b, preferred_element_type=F32)


def dot3(a, b):
    return dot(a[0], b[0]) + (dot(a[0], b[1]) + dot(a[1], b[0]))


def analysis_kernel(
    region_ref, weight_ref, new_ref, table_ref, out_ref,
    gram_ref, system_ref, inverse_ref, rows_ref,
):
    me = lax.axis_index("tile")
    rank = lax.axis_index("mem")
    ranks, tiles = table_ref.shape[0], LIVE + HPEER * HCAP
    members, capacity, width = out_ref.shape
    obs_slots = table_ref.shape[3]
    pieces = width // obs_slots
    side = ranks * PADDED
    ensemble = ranks * members
    live_count = new_ref[me + 1] - new_ref[me]

    row = lax.broadcasted_iota(jnp.int32, (side, side), 0)
    column = lax.broadcasted_iota(jnp.int32, (side, side), 1)
    real = (lax.rem(row, PADDED) < members) & (lax.rem(column, PADDED) < members)
    diagonal = (row == column).astype(F32)
    shift = jnp.where(real, diagonal * ((ensemble - 1) / INFLATION), 0.0)
    lane = lax.broadcasted_iota(jnp.int32, (1, side), 1)
    real_lane = lax.rem(lane, PADDED) < members

    def all_members(at):
        rows = [table_ref[r, at].astype(F32) for r in range(ranks)]
        return jnp.concatenate(rows, axis=0).astype(BF16)

    for t in range(tiles):
        block = all_members(t)
        gram_ref[t] = lax.dot_general(
            block, block, (((1,), (1,)), ((), ())), preferred_element_type=F32
        )

    frobenius, pull = [], []
    for i in range(LIVE):
        total = gram_ref[i]
        for e in range(region_ref.shape[0]):
            r = region_ref[e, i]
            at = jnp.where(r < capacity, jnp.minimum(r, LIVE - 1), r - capacity + LIVE)
            total = total + weight_ref[e, i] * gram_ref[at]
        pull.append(jnp.where(real_lane, total[members : members + 1, :], 0.0))
        system = jnp.where(real, total, 0.0) + shift
        squared = jnp.sum(jnp.sum(system * system, axis=0, keepdims=True), axis=1, keepdims=True)
        norm = jnp.sqrt(squared)
        frobenius.append(norm)
        root = system * (1.0 / norm)
        middle = 1.5 * diagonal - 0.5 * root
        inverse_ref[i] = middle
        system_ref[i] = dot3(split(root), split(middle))

    for step in range(1, NS_ITERS):
        for i in range(LIVE):
            root, inverse = split(system_ref[i]), split(inverse_ref[i])
            middle = split(1.5 * diagonal - 0.5 * dot3(inverse, root))
            if step < NS_ITERS - 1:
                system_ref[i] = dot3(root, middle)
            inverse_ref[i] = dot3(middle, inverse)

    own_row = lax.broadcasted_iota(jnp.int32, (PADDED, side), 0)
    for i in range(LIVE):
        inverse = split(inverse_ref[i])
        pulled = jnp.broadcast_to(pull[i], (8, side))
        half_way = dot3(split(pulled), inverse)
        mean_weight = dot3(split(half_way), inverse)[0:1, :] / frobenius[i]
        own = inverse_ref[i, pl.ds(pl.multiple_of(rank * PADDED, 8), PADDED), :]
        spread = (math.sqrt(ensemble - 1) / jnp.sqrt(frobenius[i])) * own
        transform = jnp.where((own_row < members) & real_lane, spread + mean_weight, 0.0)
        transform = transform.astype(BF16)
        keep_share = 1.0 - jnp.sum(transform.astype(F32), axis=1, keepdims=True)
        ones = jnp.where((own_row == members) & real_lane, 1.0, 0.0).astype(BF16)
        weights = transform + ones
        for c in range(pieces):
            blended = dot(weights, all_members(tiles + i * pieces + c))
            mean_state = blended[members : members + 1, :] / ensemble
            analysis = blended[:members] + keep_share[:members] * mean_state
            rows_ref[c, pl.ds(i, members, stride=PITCH), :] = jnp.where(i < live_count, analysis, 0.0)
    for i in range(LIVE, capacity):
        for c in range(pieces):
            rows_ref[c, pl.ds(i, members, stride=PITCH), :] = jnp.zeros((members, obs_slots), F32)
    for m in range(members):
        for c in range(pieces):
            span = slice(c * obs_slots, (c + 1) * obs_slots)
            out_ref[m, :, span] = rows_ref[c, m * PITCH : m * PITCH + capacity, :].astype(BF16)


def shards(
    background, obs_ens, innovation, precision, loc_weight,
    old_split, new_split, obs_count, halo_tiles, region_list,
):
    capacity, members, width = background.shape
    obs_slots = obs_ens.shape[2]
    devices = lax.axis_size("tile")
    ranks = lax.axis_size("mem")
    pieces = width // obs_slots
    tiles = LIVE + HPEER * HCAP
    smem = pl.BlockSpec(memory_space=SMEM)
    vmem = pl.BlockSpec(memory_space=VMEM)
    hbm = pl.BlockSpec(memory_space=pltpu.HBM)

    def params(mebibytes):
        return pltpu.CompilerParams(vmem_limit_bytes=mebibytes << 20)

    def tile_blocks(*leading):
        return jax.ShapeDtypeStruct((*leading, PADDED, obs_slots), BF16)

    background, obs_ens = background.transpose(1, 0, 2), obs_ens.transpose(1, 0, 2)
    halo_tiles, region_list, loc_weight = halo_tiles.T, region_list.T, loc_weight.T

    own, state, block, *swaps = pl.pallas_call(
        pack_kernel,
        out_shape=(
            tile_blocks(LIVE),
            tile_blocks(capacity, pieces),
            tile_blocks(BLOCK, HCAP + MOVE * pieces),
            tile_blocks(HCAP),
            tile_blocks(HCAP),
            tile_blocks(HCAP + MOVE * pieces),
        ),
        in_specs=[smem] * 4 + [vmem] * 4,
        out_specs=[vmem] * 6,
        scratch_shapes=[
            VMEM((members * PITCH, obs_slots), F32),
            VMEM((pieces, members * PITCH, obs_slots), F32),
        ],
        compiler_params=params(56),
    )(obs_count, old_split, new_split, halo_tiles, obs_ens, innovation, precision, background)

    groups = [list(range(b, b + BLOCK)) for b in range(0, devices, BLOCK)]
    block = lax.all_to_all(block, "tile", 0, 0, axis_index_groups=groups, tiled=True)
    arrived = []
    for swap, value in zip(SWAPS, swaps):
        pairs = [(d, d + swap[d % BLOCK]) for d in range(devices)]
        pairs = [(d, e) for d, e in pairs if 0 <= e < devices]
        arrived.append(lax.ppermute(value, "tile", pairs))

    entries = tiles + LIVE * pieces
    table = pl.pallas_call(
        table_kernel,
        out_shape=tile_blocks(ranks, entries),
        in_specs=[hbm] * 5 + [vmem] * 4,
        out_specs=pl.BlockSpec(memory_space=pl.ANY),
        scratch_shapes=[
            VMEM((entries, PADDED, obs_slots), BF16),
            VMEM((capacity, pieces, PADDED, obs_slots), BF16),
            SMEM(old_split.shape, jnp.int32),
            SMEM(new_split.shape, jnp.int32),
            SMEM(halo_tiles.shape, jnp.int32),
            pltpu.SemaphoreType.DMA((max(ranks, 5),)),
        ],
        compiler_params=params(56),
    )(old_split, new_split, halo_tiles, own, state, block, *arrived)
    table = lax.all_to_all(table, "mem", 0, 0, tiled=True)

    side = ranks * PADDED
    analysis = pl.pallas_call(
        analysis_kernel,
        out_shape=jax.ShapeDtypeStruct((members, capacity, width), BF16),
        in_specs=[smem] * 3 + [vmem],
        out_specs=vmem,
        scratch_shapes=[
            VMEM((tiles, side, side), F32),
            VMEM((LIVE, side, side), F32),
            VMEM((LIVE, side, side), F32),
            VMEM((pieces, members * PITCH, obs_slots), F32),
        ],
        compiler_params=params(28),
    )(region_list, loc_weight, new_split, table)
    return analysis.transpose(1, 0, 2)


def solution(mesh):
    in_specs = (
        P("tile", "mem", None),
        P("tile", "mem", None),
        P("tile", None),
        P("tile", None),
        P("tile", None),
        P(),
        P(),
        P("tile"),
        P(),
        P("tile", None),
    )
    out_specs = P("tile", "mem", None)
    return jax.shard_map(shards, mesh=mesh, in_specs=in_specs, out_specs=out_specs, check_vma=False)
```

```python
import functools
import math

import jax
import jax.numpy as jnp
from jax import lax
from jax.experimental import pallas as pl
from jax.experimental.pallas import tpu as pltpu
from jax.sharding import PartitionSpec as P

MOVE = 2
REACH = 3
HPEER = 3
HCAP = 4
NS_ITERS = 6
LIVE = 10
BLOCK = 4
PADDED = 24
INFLATION = 1.1
PITCH = 16

SWAPS = ((-3, 3, -3, 3), (-2, -2, 2, 2), (-1, -3, 3, 1))

SMEM = pltpu.SMEM
VMEM = pltpu.VMEM
F32 = jnp.float32
BF16 = jnp.bfloat16


def chosen(place, values):
    result = values[0]
    for k in range(1, len(values)):
        result = jnp.where(place == k, values[k], result)
    return result


def padded_rows(x, extra=()):
    rows = x.shape[0] + len(extra)
    zeros = jnp.zeros((PADDED - rows, x.shape[1]), x.dtype)
    return jnp.concatenate([x, *extra, zeros], axis=0)


def pack_kernel(
    count_ref, old_ref, new_ref, halo_ref,
    obs_ref, innovation_ref, precision_ref, background_ref,
    own_ref, state_ref, block_ref, *refs,
):
    swap_refs, (obs_rows, state_rows) = refs[:-2], refs[-2:]
    devices = new_ref.shape[0] - 1
    me = lax.axis_index("tile")
    place = lax.rem(me, BLOCK)
    new_start, new_end = new_ref[me], new_ref[me + 1]
    members, capacity, obs_slots = obs_ref.shape
    pieces = background_ref.shape[2] // obs_slots

    lane = lax.broadcasted_iota(jnp.int32, (1, obs_slots), 1)
    live = [(lane < count_ref[i]).astype(F32) for i in range(capacity)]
    root = jnp.sqrt(precision_ref[...] * jnp.concatenate(live, axis=0))
    pulled = root * innovation_ref[...]
    for m in range(members):
        obs_rows[m * PITCH : m * PITCH + capacity, :] = obs_ref[m].astype(F32) * root
        for c in range(pieces):
            span = slice(c * obs_slots, (c + 1) * obs_slots)
            state_rows[c, m * PITCH : m * PITCH + capacity, :] = background_ref[m, :, span].astype(F32)
    for i in range(LIVE):
        scaled = obs_rows[pl.ds(i, members, stride=PITCH), :]
        own_ref[i] = padded_rows(scaled, (pulled[i : i + 1, :],)).astype(BF16)
    for i in range(capacity):
        for c in range(pieces):
            rows = state_rows[c, pl.ds(i, members, stride=PITCH), :]
            state_ref[i, c] = padded_rows(rows).astype(BF16)

    def pack(reader, put):
        reader = jnp.clip(reader, 0, devices - 1)
        group = 0
        for g in range(1, HPEER):
            first = halo_ref[g * HCAP, reader]
            group = jnp.where((first >= new_start) & (first < new_end), g, group)
        for k in range(HCAP):
            row = jnp.clip(halo_ref[group * HCAP + k, reader] - new_start, 0, LIVE - 1)
            put(k, own_ref[row])

    for j in range(BLOCK):
        def put(k, value, j=j):
            block_ref[j, k] = value
        pack(me - place + j, put)
    for swap, swap_ref in zip(SWAPS, swap_refs):
        def put(k, value, swap_ref=swap_ref):
            swap_ref[k] = value
        pack(me + chosen(place, swap), put)

    old_count = old_ref[me + 1] - old_ref[me]
    for first, inside, slot in (
        (old_count - MOVE, place < BLOCK - 1, place + 1),
        (0, place > 0, place - 1),
    ):
        for t in range(MOVE):
            for c in range(pieces):
                piece = state_ref[first + t, c]
                at = HCAP + t * pieces + c

                @pl.when(inside)
                def _():
                    block_ref[slot, at] = piece

                @pl.when(jnp.logical_not(inside))
                def _():
                    swap_refs[-1][at] = piece


def table_kernel(
    old_hbm, new_hbm, halo_hbm, own_hbm, state_hbm, block_ref, *refs
):
    swap_refs, (out_ref, table_ref, state_ref, old_ref, new_ref, halo_ref, sems) = refs[:-7], refs[-7:]
    fetches = [
        pltpu.make_async_copy(source, target, sems.at[k])
        for k, (source, target) in enumerate((
            (old_hbm, old_ref),
            (new_hbm, new_ref),
            (halo_hbm, halo_ref),
            (own_hbm, table_ref.at[pl.ds(0, LIVE)]),
            (state_hbm, state_ref),
        ))
    ]
    for fetch in fetches:
        fetch.start()
    for fetch in fetches:
        fetch.wait()
    devices = new_ref.shape[0] - 1
    me = lax.axis_index("tile")
    place = lax.rem(me, BLOCK)
    base = me - place
    old_start, old_end, new_start = old_ref[me], old_ref[me + 1], new_ref[me]
    pieces = state_ref.shape[1]

    for g in range(HPEER):
        first = halo_ref[g * HCAP, me]
        peer = me - REACH
        for o in range(1 - REACH, REACH + 1):
            bound = new_ref[jnp.clip(me + o, 0, devices)]
            peer = peer + (bound <= first).astype(jnp.int32)
        at = LIVE + g * HCAP

        @pl.when((peer >= base) & (peer < base + BLOCK))
        def _():
            slot = jnp.clip(peer - base, 0, BLOCK - 1)
            for k in range(HCAP):
                table_ref[at + k] = block_ref[slot, k]

        for swap, swap_ref in zip(SWAPS, swap_refs):
            @pl.when(peer == me + chosen(place, swap))
            def _():
                for k in range(HCAP):
                    table_ref[at + k] = swap_ref[k]

    for i in range(LIVE):
        tile = new_start + i
        at = LIVE + HPEER * HCAP + i * pieces
        stays = (tile >= old_start) & (tile < old_end)
        from_left = tile < old_start
        inside = jnp.where(from_left, place > 0, place < BLOCK - 1)
        left = jnp.clip(tile - old_start + MOVE, 0, MOVE - 1)
        right = jnp.clip(tile - old_end, 0, MOVE - 1)
        begin = HCAP + jnp.where(from_left, left, right) * pieces
        slot = jnp.clip(jnp.where(from_left, place - 1, place + 1), 0, BLOCK - 1)

        @pl.when(stays)
        def _():
            own = jnp.clip(tile - old_start, 0, state_ref.shape[0] - 1)
            for c in range(pieces):
                table_ref[at + c] = state_ref[own, c]

        @pl.when(jnp.logical_not(stays) & inside)
        def _():
            for c in range(pieces):
                table_ref[at + c] = block_ref[slot, begin + c]

        @pl.when(jnp.logical_not(stays) & jnp.logical_not(inside))
        def _():
            for c in range(pieces):
                table_ref[at + c] = swap_refs[-1][begin + c]

    copies = [
        pltpu.make_async_copy(table_ref, out_ref.at[r], sems.at[r])
        for r in range(out_ref.shape[0])
    ]
    for copy in copies:
        copy.start()
    for copy in copies:
        copy.wait()


def split(x):
    high = x.astype(BF16)
    return high, (x - high.astype(F32)).astype(BF16)


def dot(a, b):
    return jnp.dot(a, b, preferred_element_type=F32)


def dot3(a, b):
    return dot(a[0], b[0]) + (dot(a[0], b[1]) + dot(a[1], b[0]))


def analysis_kernel(
    region_ref, weight_ref, new_ref, table_ref, out_ref,
    gram_ref, system_ref, inverse_ref, rows_ref,
):
    me = lax.axis_index("tile")
    rank = lax.axis_index("mem")
    ranks, tiles = table_ref.shape[0], LIVE + HPEER * HCAP
    members, capacity, width = out_ref.shape
    obs_slots = table_ref.shape[3]
    pieces = width // obs_slots
    side = ranks * PADDED
    ensemble = ranks * members
    live_count = new_ref[me + 1] - new_ref[me]

    row = lax.broadcasted_iota(jnp.int32, (side, side), 0)
    column = lax.broadcasted_iota(jnp.int32, (side, side), 1)
    real = (lax.rem(row, PADDED) < members) & (lax.rem(column, PADDED) < members)
    diagonal = (row == column).astype(F32)
    shift = jnp.where(real, diagonal * ((ensemble - 1) / INFLATION), 0.0)
    lane = lax.broadcasted_iota(jnp.int32, (1, side), 1)
    real_lane = lax.rem(lane, PADDED) < members

    def all_members(at):
        rows = [table_ref[r, at].astype(F32) for r in range(ranks)]
        return jnp.concatenate(rows, axis=0).astype(BF16)

    for t in range(tiles):
        block = all_members(t)
        gram_ref[t] = lax.dot_general(
            block, block, (((1,), (1,)), ((), ())), preferred_element_type=F32
        )

    frobenius, pull, change = [], [], []
    for i in range(LIVE):
        total = gram_ref[i]
        for e in range(region_ref.shape[0]):
            r = region_ref[e, i]
            at = jnp.where(r < capacity, jnp.minimum(r, LIVE - 1), r - capacity + LIVE)
            total = total + weight_ref[e, i] * gram_ref[at]
        pull.append(jnp.where(real_lane, total[members : members + 1, :], 0.0))
        system = jnp.where(real, total, 0.0) + shift
        squared = jnp.sum(jnp.sum(system * system, axis=0, keepdims=True), axis=1, keepdims=True)
        norm = jnp.sqrt(squared)
        frobenius.append(norm)
        root = system * (1.0 / norm)
        half = 0.5 * (diagonal - root)
        system_ref[i] = root
        inverse_ref[i] = diagonal + half
        change.append(split(half))

    for step in range(NS_ITERS):
        if step:
            change = []
            for i in range(LIVE):
                product = dot3(split(inverse_ref[i]), split(system_ref[i]))
                change.append(split(0.5 * (diagonal - product)))
        for i in range(LIVE):
            if step:
                inverse = inverse_ref[i]
                inverse_ref[i] = inverse + dot3(change[i], split(inverse))
            if step < NS_ITERS - 1:
                root = system_ref[i]
                system_ref[i] = root + dot3(split(root), change[i])

    own_row = lax.broadcasted_iota(jnp.int32, (PADDED, side), 0)
    inverses = [split(inverse_ref[i]) for i in range(LIVE)]
    half_way = [
        dot3(split(jnp.broadcast_to(pull[i], (8, side))), inverses[i]) for i in range(LIVE)
    ]
    mean_weights = [dot3(split(half_way[i]), inverses[i])[0:1, :] for i in range(LIVE)]
    for i in range(LIVE):
        mean_weight = mean_weights[i] * (1.0 / frobenius[i])
        own = inverse_ref[i, pl.ds(pl.multiple_of(rank * PADDED, 8), PADDED), :]
        spread = (math.sqrt(ensemble - 1) * lax.rsqrt(frobenius[i])) * own
        transform = jnp.where((own_row < members) & real_lane, spread + mean_weight, 0.0)
        transform = transform.astype(BF16)
        keep_share = 1.0 - jnp.sum(transform.astype(F32), axis=1, keepdims=True)
        weights = transform + jnp.where((own_row == members) & real_lane, 1.0, 0.0).astype(BF16)
        for c in range(pieces):
            blended = dot(weights, all_members(tiles + i * pieces + c))
            mean_state = blended[members : members + 1, :] / ensemble
            analysis = blended[:members] + keep_share[:members] * mean_state
            rows_ref[c, pl.ds(i, members, stride=PITCH), :] = jnp.where(i < live_count, analysis, 0.0)
    for i in range(LIVE, capacity):
        for c in range(pieces):
            rows_ref[c, pl.ds(i, members, stride=PITCH), :] = jnp.zeros((members, obs_slots), F32)
    for m in range(members):
        for c in range(pieces):
            span = slice(c * obs_slots, (c + 1) * obs_slots)
            out_ref[m, :, span] = rows_ref[c, m * PITCH : m * PITCH + capacity, :].astype(BF16)


def shards(
    background, obs_ens, innovation, precision, loc_weight,
    old_split, new_split, obs_count, halo_tiles, region_list,
):
    capacity, members, width = background.shape
    obs_slots = obs_ens.shape[2]
    devices = lax.axis_size("tile")
    ranks = lax.axis_size("mem")
    pieces = width // obs_slots
    tiles = LIVE + HPEER * HCAP
    smem = pl.BlockSpec(memory_space=SMEM)
    vmem = pl.BlockSpec(memory_space=VMEM)
    hbm = pl.BlockSpec(memory_space=pltpu.HBM)

    def params(mebibytes):
        return pltpu.CompilerParams(vmem_limit_bytes=mebibytes << 20)

    def tile_blocks(*leading):
        return jax.ShapeDtypeStruct((*leading, PADDED, obs_slots), BF16)

    background, obs_ens = background.transpose(1, 0, 2), obs_ens.transpose(1, 0, 2)
    halo_tiles, region_list, loc_weight = halo_tiles.T, region_list.T, loc_weight.T

    own, state, block, *swaps = pl.pallas_call(
        pack_kernel,
        out_shape=(
            tile_blocks(LIVE),
            tile_blocks(capacity, pieces),
            tile_blocks(BLOCK, HCAP + MOVE * pieces),
            tile_blocks(HCAP),
            tile_blocks(HCAP),
            tile_blocks(HCAP + MOVE * pieces),
        ),
        in_specs=[smem] * 4 + [vmem] * 4,
        out_specs=[vmem] * 6,
        scratch_shapes=[
            VMEM((members * PITCH, obs_slots), F32),
            VMEM((pieces, members * PITCH, obs_slots), F32),
        ],
        compiler_params=params(56),
    )(obs_count, old_split, new_split, halo_tiles, obs_ens, innovation, precision, background)

    groups = [list(range(b, b + BLOCK)) for b in range(0, devices, BLOCK)]
    block = lax.all_to_all(block, "tile", 0, 0, axis_index_groups=groups, tiled=True)
    arrived = []
    for swap, value in zip(SWAPS, swaps):
        pairs = [(d, d + swap[d % BLOCK]) for d in range(devices)]
        pairs = [(d, e) for d, e in pairs if 0 <= e < devices]
        arrived.append(lax.ppermute(value, "tile", pairs))

    entries = tiles + LIVE * pieces
    table = pl.pallas_call(
        table_kernel,
        out_shape=tile_blocks(ranks, entries),
        in_specs=[hbm] * 5 + [vmem] * 4,
        out_specs=pl.BlockSpec(memory_space=pl.ANY),
        scratch_shapes=[
            VMEM((entries, PADDED, obs_slots), BF16),
            VMEM((capacity, pieces, PADDED, obs_slots), BF16),
            SMEM(old_split.shape, jnp.int32),
            SMEM(new_split.shape, jnp.int32),
            SMEM(halo_tiles.shape, jnp.int32),
            pltpu.SemaphoreType.DMA((max(ranks, 5),)),
        ],
        compiler_params=params(56),
    )(old_split, new_split, halo_tiles, own, state, block, *arrived)
    table = lax.all_to_all(table, "mem", 0, 0, tiled=True)

    side = ranks * PADDED
    analysis = pl.pallas_call(
        analysis_kernel,
        out_shape=jax.ShapeDtypeStruct((members, capacity, width), BF16),
        in_specs=[smem] * 3 + [vmem],
        out_specs=vmem,
        scratch_shapes=[
            VMEM((tiles, side, side), F32),
            VMEM((LIVE, side, side), F32),
            VMEM((LIVE, side, side), F32),
            VMEM((pieces, members * PITCH, obs_slots), F32),
        ],
        compiler_params=params(28),
    )(region_list, loc_weight, new_split, table)
    return analysis.transpose(1, 0, 2)


def solution(mesh):
    in_specs = (
        P("tile", "mem", None),
        P("tile", "mem", None),
        P("tile", None),
        P("tile", None),
        P("tile", None),
        P(),
        P(),
        P("tile"),
        P(),
        P("tile", None),
    )
    out_specs = P("tile", "mem", None)
    return jax.shard_map(shards, mesh=mesh, in_specs=in_specs, out_specs=out_specs, check_vma=False)
```

```python
import functools
import math

import jax
import jax.numpy as jnp
from jax import lax
from jax.experimental import pallas as pl
from jax.experimental.pallas import tpu as pltpu
from jax.sharding import PartitionSpec as P

MOVE = 2
REACH = 3
HPEER = 3
HCAP = 4
NS_ITERS = 6
LIVE = 10
BLOCK = 4
PADDED = 24
INFLATION = 1.1
COST = pl.CostEstimate(flops=1 << 20, bytes_accessed=4 << 20, transcendentals=0)
PITCH = 16

SWAPS = ((-3, 3, -3, 3), (-2, -2, 2, 2), (-1, -3, 3, 1))

SMEM = pltpu.SMEM
VMEM = pltpu.VMEM
F32 = jnp.float32
BF16 = jnp.bfloat16


def chosen(place, values):
    result = values[0]
    for k in range(1, len(values)):
        result = jnp.where(place == k, values[k], result)
    return result


def padded_to(x, rows):
    return jnp.concatenate([x, jnp.zeros((rows - x.shape[0], x.shape[1]), x.dtype)], axis=0)


def paired(x, y):
    return jnp.concatenate([x.astype(F32), y.astype(F32)], axis=0).astype(BF16)


def pack_kernel(
    count_ref, old_ref, new_ref, halo_ref,
    obs_ref, innovation_ref, precision_ref, background_ref,
    own_ref, pulled_ref, block_ref, *refs,
):
    swap_refs, (obs_rows, state_rows) = refs[:-2], refs[-2:]
    devices = new_ref.shape[0] - 1
    me = lax.axis_index("tile")
    place = lax.rem(me, BLOCK)
    new_start, new_end = new_ref[me], new_ref[me + 1]
    members, capacity, obs_slots = obs_ref.shape
    pieces = background_ref.shape[2] // obs_slots

    lane = lax.broadcasted_iota(jnp.int32, (1, obs_slots), 1)
    live = [(lane < count_ref[i]).astype(F32) for i in range(capacity)]
    root = jnp.sqrt(precision_ref[...] * jnp.concatenate(live, axis=0))
    pulled = root * innovation_ref[...]
    for m in range(members):
        obs_rows[m * PITCH : m * PITCH + capacity, :] = obs_ref[m].astype(F32) * root
        for c in range(pieces):
            span = slice(c * obs_slots, (c + 1) * obs_slots)
            state_rows[c, m * PITCH : m * PITCH + capacity, :] = background_ref[m, :, span].astype(F32)
    pulled_ref[...] = padded_to(pulled, PITCH).astype(BF16).astype(F32)
    for i in range(LIVE):
        scaled = obs_rows[pl.ds(i, members, stride=PITCH), :]
        own_ref[i] = padded_to(jnp.concatenate([scaled, pulled[i : i + 1, :]], axis=0), PADDED).astype(BF16)

    def pack(reader, put):
        reader = jnp.clip(reader, 0, devices - 1)
        group = 0
        for g in range(1, HPEER):
            first = halo_ref[g * HCAP, reader]
            group = jnp.where((first >= new_start) & (first < new_end), g, group)
        for k in range(HCAP):
            row = jnp.clip(halo_ref[group * HCAP + k, reader] - new_start, 0, LIVE - 1)
            put(k, own_ref[row])

    for j in range(BLOCK):
        def put(k, value, j=j):
            block_ref[j, k] = value
        pack(me - place + j, put)
    for swap, swap_ref in zip(SWAPS, swap_refs):
        def put(k, value, swap_ref=swap_ref):
            swap_ref[k] = value
        pack(me + chosen(place, swap), put)

    old_count = old_ref[me + 1] - old_ref[me]
    for first, inside, slot in (
        (old_count - MOVE, place < BLOCK - 1, place + 1),
        (0, place > 0, place - 1),
    ):
        for t in range(MOVE):
            for c in range(pieces):
                piece = state_rows[c, pl.ds(first + t, members, stride=PITCH), :]
                piece = padded_to(piece, PADDED).astype(BF16)
                at = HCAP + t * pieces + c

                @pl.when(inside)
                def _():
                    block_ref[slot, at] = piece

                @pl.when(jnp.logical_not(inside))
                def _():
                    swap_refs[-1][at] = piece


def own_table_kernel(
    old_ref, new_ref, own_ref, background_ref, out_ref, table_ref, state_rows, sems
):
    me = lax.axis_index("tile")
    old_start, old_end, new_start = old_ref[me], old_ref[me + 1], new_ref[me]
    members, capacity, width = background_ref.shape
    obs_slots = own_ref.shape[2]
    pieces = width // obs_slots
    for m in range(members):
        for c in range(pieces):
            span = slice(c * obs_slots, (c + 1) * obs_slots)
            state_rows[c, m * PITCH : m * PITCH + capacity, :] = background_ref[m, :, span].astype(F32)
    for i in range(0, LIVE, 2):
        table_ref[i // 2] = paired(own_ref[i][:members], own_ref[i + 1][:members])
    for i in range(LIVE):
        at = jnp.clip(new_start + i - old_start, 0, capacity - 1)
        rows = [state_rows[c, pl.ds(at, members, stride=PITCH), :] for c in range(pieces)]
        for c in range(0, pieces, 2):
            table_ref[(LIVE + HPEER * HCAP + i * pieces + c) // 2] = paired(rows[c], rows[c + 1])
    copies = [
        pltpu.make_async_copy(table_ref, out_ref.at[r], sems.at[r])
        for r in range(out_ref.shape[0])
    ]
    for copy in copies:
        copy.start()
    for copy in copies:
        copy.wait()


def table_kernel(old_ref, new_ref, halo_ref, table_ref, block_ref, *refs):
    swap_refs, (out_ref, pulled_ref, halo_rows, moved_rows, halo_sems, moved_sems) = refs[:-6], refs[-6:]
    devices = new_ref.shape[0] - 1
    me = lax.axis_index("tile")
    place = lax.rem(me, BLOCK)
    base = me - place
    old_start, old_end = old_ref[me], old_ref[me + 1]
    new_start, new_end = new_ref[me], new_ref[me + 1]
    ranks, _, pair_rows, _ = out_ref.shape
    members = pair_rows // 2
    pieces = (block_ref.shape[1] - HCAP) // MOVE
    pulled_ref[...] = jnp.zeros(pulled_ref.shape, F32)

    moves = []
    for j in range(MOVE):
        tile = new_start + j
        index = jnp.clip(tile - old_start + MOVE, 0, MOVE - 1)
        moves.append((tile < old_start, j, index, place > 0, place - 1))
    for j in range(MOVE):
        tile = old_end + j
        slot = jnp.clip(tile - new_start, 0, LIVE - 1)
        moves.append((tile < new_end, slot, j, place < BLOCK - 1, place + 1))
    copies = []
    for n, (comes, slot, index, inside, source) in enumerate(moves):
        begin = HCAP + index * pieces
        source = jnp.clip(source, 0, BLOCK - 1)
        at = (LIVE + HPEER * HCAP + slot * pieces) // 2
        mine = [
            pltpu.make_async_copy(
                moved_rows.at[n], out_ref.at[r, pl.ds(at, pieces // 2)], moved_sems.at[n, r]
            )
            for r in range(ranks)
        ]
        copies.append((comes, mine))

        def put(read, n=n):
            for c in range(0, pieces, 2):
                moved_rows[n, c // 2] = paired(read(c)[:members], read(c + 1)[:members])

        @pl.when(comes & inside)
        def _():
            put(lambda c: block_ref[source, begin + c])

        @pl.when(comes & jnp.logical_not(inside))
        def _():
            put(lambda c: swap_refs[-1][begin + c])

        @pl.when(comes)
        def _():
            for copy in mine:
                copy.start()

    for g in range(HPEER):
        first = halo_ref[g * HCAP, me]
        peer = me - REACH
        for o in range(1 - REACH, REACH + 1):
            bound = new_ref[jnp.clip(me + o, 0, devices)]
            peer = peer + (bound <= first).astype(jnp.int32)

        def put(read, g=g):
            for k in range(HCAP):
                at = g * HCAP + k
                pulled_ref[at : at + 1, :] = read(k).astype(F32)[members : members + 1]
            for k in range(0, HCAP, 2):
                halo_rows[(g * HCAP + k) // 2] = paired(read(k)[:members], read(k + 1)[:members])

        @pl.when((peer >= base) & (peer < base + BLOCK))
        def _():
            slot = jnp.clip(peer - base, 0, BLOCK - 1)
            put(lambda k: block_ref[slot, k])

        for swap, swap_ref in zip(SWAPS, swap_refs):
            @pl.when(peer == me + chosen(place, swap))
            def _():
                put(lambda k: swap_ref[k])

    halo = [
        pltpu.make_async_copy(
            halo_rows, out_ref.at[r, pl.ds(LIVE // 2, HPEER * HCAP // 2)], halo_sems.at[r]
        )
        for r in range(ranks)
    ]
    for copy in halo:
        copy.start()
    for comes, mine in copies:
        @pl.when(comes)
        def _():
            for copy in mine:
                copy.wait()
    for copy in halo:
        copy.wait()


def split(x):
    high = x.astype(BF16)
    return high, (x - high.astype(F32)).astype(BF16)


def dot(a, b):
    return jnp.dot(a, b, preferred_element_type=F32)


def dot3(a, b):
    return dot(a[0], b[0]) + (dot(a[0], b[1]) + dot(a[1], b[0]))


def analysis_kernel(
    region_ref, weight_ref, new_ref, own_pulled_ref, halo_pulled_ref, table_ref, out_ref,
    gram_ref, system_ref, inverse_ref, rows_ref,
):
    me = lax.axis_index("tile")
    rank = lax.axis_index("mem")
    ranks, tiles = table_ref.shape[0], LIVE + HPEER * HCAP
    members, capacity, width = out_ref.shape
    obs_slots = table_ref.shape[3]
    pieces = width // obs_slots
    side = ranks * members
    live_count = new_ref[me + 1] - new_ref[me]

    row = lax.broadcasted_iota(jnp.int32, (side, side), 0)
    column = lax.broadcasted_iota(jnp.int32, (side, side), 1)
    diagonal = (row == column).astype(F32)
    shift = diagonal * ((side - 1) / INFLATION)

    def all_members(pair):
        rows = [table_ref[r, pair].astype(F32) for r in range(ranks)]
        return [
            jnp.concatenate([x[k * members : (k + 1) * members] for x in rows], axis=0).astype(BF16)
            for k in range(2)
        ]

    for t in range(0, tiles, 2):
        for k, block in enumerate(all_members(t // 2)):
            at = t + k
            pulled_ref, where = (own_pulled_ref, at) if at < LIVE else (halo_pulled_ref, at - LIVE)
            pulled = padded_to(pulled_ref[where : where + 1, :], PITCH).astype(BF16)
            product = lax.dot_general(
                jnp.concatenate([block, pulled], axis=0), block,
                (((1,), (1,)), ((), ())), preferred_element_type=F32,
            )
            gram_ref[at] = product[: side + 8]

    frobenius, pull, change = [], [], []
    for i in range(LIVE):
        total = gram_ref[i]
        for e in range(region_ref.shape[0]):
            r = region_ref[e, i]
            at = jnp.where(r < capacity, jnp.minimum(r, LIVE - 1), r - capacity + LIVE)
            total = total + weight_ref[e, i] * gram_ref[at]
        pull.append(total[side : side + 1, :])
        system = total[:side] + shift
        squared = jnp.sum(jnp.sum(system * system, axis=0, keepdims=True), axis=1, keepdims=True)
        norm = jnp.sqrt(squared)
        frobenius.append(norm)
        root = system * (1.0 / norm)
        half = 0.5 * (diagonal - root)
        system_ref[i] = root
        inverse_ref[i] = diagonal + half
        change.append(split(half))

    for step in range(NS_ITERS):
        if step:
            change = []
            for i in range(LIVE):
                product = dot3(split(inverse_ref[i]), split(system_ref[i]))
                change.append(split(0.5 * (diagonal - product)))
        for i in range(LIVE):
            if step:
                inverse = inverse_ref[i]
                inverse_ref[i] = inverse + dot3(change[i], split(inverse))
            if step < NS_ITERS - 1:
                root = system_ref[i]
                system_ref[i] = root + dot3(split(root), change[i])

    start = pl.multiple_of(rank * members // 8 * 8, 8)
    begins_inside = rank * members > start
    ones = jnp.ones((1, side), F32)
    inverses = [split(inverse_ref[i]) for i in range(LIVE)]
    half_way = [
        dot3(split(jnp.broadcast_to(pull[i], (8, side))), inverses[i]) for i in range(LIVE)
    ]
    mean_weights = [dot3(split(half_way[i]), inverses[i])[0:1, :] for i in range(LIVE)]
    for i in range(LIVE):
        mean_weight = mean_weights[i] * (1.0 / frobenius[i])
        own = inverse_ref[i, pl.ds(start, PADDED), :]
        own = jnp.where(begins_inside, own[PADDED - members :], own[:members])
        transform = (math.sqrt(side - 1) * lax.rsqrt(frobenius[i])) * own + mean_weight
        transform = transform.astype(BF16).astype(F32)
        keep_share = 1.0 - jnp.sum(transform, axis=1, keepdims=True)
        weights = padded_to(jnp.concatenate([transform, ones], axis=0), 2 * PITCH).astype(BF16)
        state = [x for c in range(0, pieces, 2) for x in all_members((tiles + i * pieces + c) // 2)]
        for c in range(pieces):
            blended = dot(weights, state[c])
            mean_state = blended[members : members + 1, :] / side
            analysis = blended[:members] + keep_share * mean_state
            rows_ref[c, pl.ds(i, members, stride=PITCH), :] = jnp.where(i < live_count, analysis, 0.0)
    for i in range(LIVE, capacity):
        for c in range(pieces):
            rows_ref[c, pl.ds(i, members, stride=PITCH), :] = jnp.zeros((members, obs_slots), F32)
    for m in range(members):
        for c in range(pieces):
            span = slice(c * obs_slots, (c + 1) * obs_slots)
            out_ref[m, :, span] = rows_ref[c, m * PITCH : m * PITCH + capacity, :].astype(BF16)


def shards(
    background, obs_ens, innovation, precision, loc_weight,
    old_split, new_split, obs_count, halo_tiles, region_list,
):
    capacity, members, width = background.shape
    obs_slots = obs_ens.shape[2]
    devices = lax.axis_size("tile")
    ranks = lax.axis_size("mem")
    pieces = width // obs_slots
    tiles = LIVE + HPEER * HCAP
    smem = pl.BlockSpec(memory_space=SMEM)
    vmem = pl.BlockSpec(memory_space=VMEM)
    hbm = pl.BlockSpec(memory_space=pltpu.HBM)

    def params(mebibytes):
        return pltpu.CompilerParams(vmem_limit_bytes=mebibytes << 20)

    def tile_blocks(*leading):
        return jax.ShapeDtypeStruct((*leading, PADDED, obs_slots), BF16)

    background, obs_ens = background.transpose(1, 0, 2), obs_ens.transpose(1, 0, 2)
    halo_tiles, region_list, loc_weight = halo_tiles.T, region_list.T, loc_weight.T

    own, own_pulled, block, *swaps = pl.pallas_call(
        pack_kernel,
        out_shape=(
            tile_blocks(LIVE),
            jax.ShapeDtypeStruct((PITCH, obs_slots), F32),
            tile_blocks(BLOCK, HCAP + MOVE * pieces),
            tile_blocks(HCAP),
            tile_blocks(HCAP),
            tile_blocks(HCAP + MOVE * pieces),
        ),
        in_specs=[smem] * 4 + [vmem] * 4,
        out_specs=[vmem] * 6,
        scratch_shapes=[
            VMEM((members * PITCH, obs_slots), F32),
            VMEM((pieces, members * PITCH, obs_slots), F32),
        ],
        compiler_params=params(56),
    )(obs_count, old_split, new_split, halo_tiles, obs_ens, innovation, precision, background)

    groups = [list(range(b, b + BLOCK)) for b in range(0, devices, BLOCK)]
    block = lax.all_to_all(block, "tile", 0, 0, axis_index_groups=groups, tiled=True)
    arrived = []
    for swap, value in zip(SWAPS, swaps):
        pairs = [(d, d + swap[d % BLOCK]) for d in range(devices)]
        pairs = [(d, e) for d, e in pairs if 0 <= e < devices]
        arrived.append(lax.ppermute(value, "tile", pairs))

    table_shape = (ranks, (tiles + LIVE * pieces) // 2, 2 * members, obs_slots)
    table = pl.pallas_call(
        own_table_kernel,
        out_shape=jax.ShapeDtypeStruct(table_shape, BF16),
        in_specs=[smem] * 2 + [vmem] * 2,
        out_specs=pl.BlockSpec(memory_space=pl.ANY),
        scratch_shapes=[
            VMEM(table_shape[1:], BF16),
            VMEM((pieces, members * PITCH, obs_slots), F32),
            pltpu.SemaphoreType.DMA((ranks,)),
        ],
        compiler_params=params(56),
        cost_estimate=COST,
    )(old_split, new_split, own, background)
    table, halo_pulled = pl.pallas_call(
        table_kernel,
        out_shape=(
            jax.ShapeDtypeStruct(table_shape, BF16),
            jax.ShapeDtypeStruct((PITCH, obs_slots), F32),
        ),
        in_specs=[smem] * 3 + [pl.BlockSpec(memory_space=pl.ANY)] + [vmem] * 4,
        out_specs=(pl.BlockSpec(memory_space=pl.ANY), vmem),
        input_output_aliases={3: 0},
        scratch_shapes=[
            VMEM((HPEER * HCAP // 2, 2 * members, obs_slots), BF16),
            VMEM((2 * MOVE, pieces // 2, 2 * members, obs_slots), BF16),
            pltpu.SemaphoreType.DMA((ranks,)),
            pltpu.SemaphoreType.DMA((2 * MOVE, ranks)),
        ],
        compiler_params=params(56),
    )(old_split, new_split, halo_tiles, table, block, *arrived)
    table = lax.all_to_all(table, "mem", 0, 0, tiled=True)

    side = ranks * members
    analysis = pl.pallas_call(
        analysis_kernel,
        out_shape=jax.ShapeDtypeStruct((members, capacity, width), BF16),
        in_specs=[smem] * 3 + [vmem] * 3,
        out_specs=vmem,
        scratch_shapes=[
            VMEM((tiles, side + 8, side), F32),
            VMEM((LIVE, side, side), F32),
            VMEM((LIVE, side, side), F32),
            VMEM((pieces, members * PITCH, obs_slots), F32),
        ],
        compiler_params=params(28),
    )(region_list, loc_weight, new_split, own_pulled, halo_pulled, table)
    return analysis.transpose(1, 0, 2)


def solution(mesh):
    in_specs = (
        P("tile", "mem", None),
        P("tile", "mem", None),
        P("tile", None),
        P("tile", None),
        P("tile", None),
        P(),
        P(),
        P("tile"),
        P(),
        P("tile", None),
    )
    out_specs = P("tile", "mem", None)
    return jax.shard_map(shards, mesh=mesh, in_specs=in_specs, out_specs=out_specs, check_vma=False)
```

```python
import functools
import math

import jax
import jax.numpy as jnp
from jax import lax
from jax.experimental import pallas as pl
from jax.experimental.pallas import tpu as pltpu
from jax.sharding import PartitionSpec as P

MOVE = 2
REACH = 3
HPEER = 3
HCAP = 4
NS_ITERS = 6
LIVE = 10
BLOCK = 4
PADDED = 24
INFLATION = 1.1
COST = pl.CostEstimate(flops=1 << 20, bytes_accessed=4 << 20, transcendentals=0)
PITCH = 16

SWAPS = ((-3, 3, -3, 3), (-2, -2, 2, 2), (-1, -3, 3, 1))

SMEM = pltpu.SMEM
VMEM = pltpu.VMEM
F32 = jnp.float32
BF16 = jnp.bfloat16


def chosen(place, values):
    result = values[0]
    for k in range(1, len(values)):
        result = jnp.where(place == k, values[k], result)
    return result


def padded_to(x, rows):
    return jnp.concatenate([x, jnp.zeros((rows - x.shape[0], x.shape[1]), x.dtype)], axis=0)


def paired(x, y):
    x, y = x.astype(F32), y.astype(F32)
    parts = [x[:PITCH], y[:PITCH], x[PITCH:], y[PITCH:]]
    return jnp.concatenate(parts, axis=0).astype(BF16)


def pack_kernel(
    count_ref, old_ref, new_ref, halo_ref,
    obs_ref, innovation_ref, precision_ref, background_ref,
    own_ref, pulled_ref, block_ref, *refs,
):
    swap_refs, (obs_rows, state_rows) = refs[:-2], refs[-2:]
    devices = new_ref.shape[0] - 1
    me = lax.axis_index("tile")
    place = lax.rem(me, BLOCK)
    new_start, new_end = new_ref[me], new_ref[me + 1]
    members, capacity, obs_slots = obs_ref.shape
    pieces = background_ref.shape[2] // obs_slots

    lane = lax.broadcasted_iota(jnp.int32, (1, obs_slots), 1)
    live = [(lane < count_ref[i]).astype(F32) for i in range(capacity)]
    root = jnp.sqrt(precision_ref[...] * jnp.concatenate(live, axis=0))
    pulled = root * innovation_ref[...]
    for m in range(members):
        obs_rows[m * PITCH : m * PITCH + capacity, :] = obs_ref[m].astype(F32) * root
        for c in range(pieces):
            span = slice(c * obs_slots, (c + 1) * obs_slots)
            state_rows[c, m * PITCH : m * PITCH + capacity, :] = background_ref[m, :, span].astype(F32)
    pulled_ref[...] = padded_to(pulled, PITCH).astype(BF16).astype(F32)
    for i in range(LIVE):
        scaled = obs_rows[pl.ds(i, members, stride=PITCH), :]
        own_ref[i] = padded_to(jnp.concatenate([scaled, pulled[i : i + 1, :]], axis=0), PADDED).astype(BF16)

    def pack(reader, put):
        reader = jnp.clip(reader, 0, devices - 1)
        group = 0
        for g in range(1, HPEER):
            first = halo_ref[g * HCAP, reader]
            group = jnp.where((first >= new_start) & (first < new_end), g, group)
        for k in range(HCAP):
            row = jnp.clip(halo_ref[group * HCAP + k, reader] - new_start, 0, LIVE - 1)
            put(k, own_ref[row])

    for j in range(BLOCK):
        def put(k, value, j=j):
            block_ref[j, k] = value
        pack(me - place + j, put)
    for swap, swap_ref in zip(SWAPS, swap_refs):
        def put(k, value, swap_ref=swap_ref):
            swap_ref[k] = value
        pack(me + chosen(place, swap), put)

    old_count = old_ref[me + 1] - old_ref[me]
    for first, inside, slot in (
        (old_count - MOVE, place < BLOCK - 1, place + 1),
        (0, place > 0, place - 1),
    ):
        for t in range(MOVE):
            for c in range(pieces):
                piece = state_rows[c, pl.ds(first + t, members, stride=PITCH), :]
                piece = padded_to(piece, PADDED).astype(BF16)
                at = HCAP + t * pieces + c

                @pl.when(inside)
                def _():
                    block_ref[slot, at] = piece

                @pl.when(jnp.logical_not(inside))
                def _():
                    swap_refs[-1][at] = piece


def own_table_kernel(
    old_ref, new_ref, own_ref, background_ref, out_ref, table_ref, state_rows, sems
):
    me = lax.axis_index("tile")
    old_start, old_end, new_start = old_ref[me], old_ref[me + 1], new_ref[me]
    members, capacity, width = background_ref.shape
    obs_slots = own_ref.shape[2]
    pieces = width // obs_slots
    for m in range(members):
        for c in range(pieces):
            span = slice(c * obs_slots, (c + 1) * obs_slots)
            state_rows[c, m * PITCH : m * PITCH + capacity, :] = background_ref[m, :, span].astype(F32)
    for i in range(0, LIVE, 2):
        table_ref[i // 2] = paired(own_ref[i][:members], own_ref[i + 1][:members])
    for i in range(LIVE):
        at = jnp.clip(new_start + i - old_start, 0, capacity - 1)
        rows = [state_rows[c, pl.ds(at, members, stride=PITCH), :] for c in range(pieces)]
        for c in range(0, pieces, 2):
            table_ref[(LIVE + HPEER * HCAP + i * pieces + c) // 2] = paired(rows[c], rows[c + 1])
    copies = [
        pltpu.make_async_copy(table_ref, out_ref.at[r], sems.at[r])
        for r in range(out_ref.shape[0])
    ]
    for copy in copies:
        copy.start()
    for copy in copies:
        copy.wait()


def table_kernel(old_ref, new_ref, halo_ref, table_ref, block_ref, *refs):
    swap_refs, (out_ref, pulled_ref, halo_rows, moved_rows, halo_sems, moved_sems) = refs[:-6], refs[-6:]
    devices = new_ref.shape[0] - 1
    me = lax.axis_index("tile")
    place = lax.rem(me, BLOCK)
    base = me - place
    old_start, old_end = old_ref[me], old_ref[me + 1]
    new_start, new_end = new_ref[me], new_ref[me + 1]
    ranks, _, pair_rows, _ = out_ref.shape
    members = pair_rows // 2
    pieces = (block_ref.shape[1] - HCAP) // MOVE
    pulled_ref[...] = jnp.zeros(pulled_ref.shape, F32)

    moves = []
    for j in range(MOVE):
        tile = new_start + j
        index = jnp.clip(tile - old_start + MOVE, 0, MOVE - 1)
        moves.append((tile < old_start, j, index, place > 0, place - 1))
    for j in range(MOVE):
        tile = old_end + j
        slot = jnp.clip(tile - new_start, 0, LIVE - 1)
        moves.append((tile < new_end, slot, j, place < BLOCK - 1, place + 1))
    copies = []
    for n, (comes, slot, index, inside, source) in enumerate(moves):
        begin = HCAP + index * pieces
        source = jnp.clip(source, 0, BLOCK - 1)
        at = (LIVE + HPEER * HCAP + slot * pieces) // 2
        mine = [
            pltpu.make_async_copy(
                moved_rows.at[n], out_ref.at[r, pl.ds(at, pieces // 2)], moved_sems.at[n, r]
            )
            for r in range(ranks)
        ]
        copies.append((comes, mine))

        def put(read, n=n):
            for c in range(0, pieces, 2):
                moved_rows[n, c // 2] = paired(read(c)[:members], read(c + 1)[:members])

        @pl.when(comes & inside)
        def _():
            put(lambda c: block_ref[source, begin + c])

        @pl.when(comes & jnp.logical_not(inside))
        def _():
            put(lambda c: swap_refs[-1][begin + c])

        @pl.when(comes)
        def _():
            for copy in mine:
                copy.start()

    for g in range(HPEER):
        first = halo_ref[g * HCAP, me]
        peer = me - REACH
        for o in range(1 - REACH, REACH + 1):
            bound = new_ref[jnp.clip(me + o, 0, devices)]
            peer = peer + (bound <= first).astype(jnp.int32)

        def put(read, g=g):
            for k in range(HCAP):
                at = g * HCAP + k
                pulled_ref[at : at + 1, :] = read(k).astype(F32)[members : members + 1]
            for k in range(0, HCAP, 2):
                halo_rows[(g * HCAP + k) // 2] = paired(read(k)[:members], read(k + 1)[:members])

        @pl.when((peer >= base) & (peer < base + BLOCK))
        def _():
            slot = jnp.clip(peer - base, 0, BLOCK - 1)
            put(lambda k: block_ref[slot, k])

        for swap, swap_ref in zip(SWAPS, swap_refs):
            @pl.when(peer == me + chosen(place, swap))
            def _():
                put(lambda k: swap_ref[k])

    halo = [
        pltpu.make_async_copy(
            halo_rows, out_ref.at[r, pl.ds(LIVE // 2, HPEER * HCAP // 2)], halo_sems.at[r]
        )
        for r in range(ranks)
    ]
    for copy in halo:
        copy.start()
    for comes, mine in copies:
        @pl.when(comes)
        def _():
            for copy in mine:
                copy.wait()
    for copy in halo:
        copy.wait()


def split(x):
    high = x.astype(BF16)
    return high, (x - high.astype(F32)).astype(BF16)


def dot(a, b):
    return jnp.dot(a, b, preferred_element_type=F32)


def dot3(a, b):
    return dot(a[0], b[0]) + (dot(a[0], b[1]) + dot(a[1], b[0]))


def analysis_kernel(
    region_ref, weight_ref, new_ref, own_pulled_ref, halo_pulled_ref, table_ref, out_ref,
    gram_ref, system_ref, inverse_ref, rows_ref,
):
    me = lax.axis_index("tile")
    rank = lax.axis_index("mem")
    ranks, tiles = table_ref.shape[0], LIVE + HPEER * HCAP
    members, capacity, width = out_ref.shape
    obs_slots = table_ref.shape[3]
    pieces = width // obs_slots
    side = ranks * members
    live_count = new_ref[me + 1] - new_ref[me]

    row = lax.broadcasted_iota(jnp.int32, (side, side), 0)
    column = lax.broadcasted_iota(jnp.int32, (side, side), 1)
    diagonal = (row == column).astype(F32)
    shift = diagonal * ((side - 1) / INFLATION)

    rest = members - PITCH

    def all_members(pair):
        rows = [table_ref[r, pair].astype(F32) for r in range(ranks)]
        blocks = []
        for k in range(2):
            parts = [x[k * PITCH : (k + 1) * PITCH] for x in rows]
            begin = 2 * PITCH + k * rest
            parts += [x[begin : begin + rest] for x in rows]
            blocks.append(jnp.concatenate(parts, axis=0).astype(BF16))
        return blocks

    for t in range(0, tiles, 2):
        for k, block in enumerate(all_members(t // 2)):
            at = t + k
            pulled_ref, where = (own_pulled_ref, at) if at < LIVE else (halo_pulled_ref, at - LIVE)
            pulled = padded_to(pulled_ref[where : where + 1, :], PITCH).astype(BF16)
            product = lax.dot_general(
                jnp.concatenate([block, pulled], axis=0), block,
                (((1,), (1,)), ((), ())), preferred_element_type=F32,
            )
            gram_ref[at] = product[: side + 8]

    frobenius, pull, change = [], [], []
    for i in range(LIVE):
        total = gram_ref[i]
        for e in range(region_ref.shape[0]):
            r = region_ref[e, i]
            at = jnp.where(r < capacity, jnp.minimum(r, LIVE - 1), r - capacity + LIVE)
            total = total + weight_ref[e, i] * gram_ref[at]
        pull.append(total[side : side + 1, :])
        system = total[:side] + shift
        squared = jnp.sum(jnp.sum(system * system, axis=0, keepdims=True), axis=1, keepdims=True)
        norm = jnp.sqrt(squared)
        frobenius.append(norm)
        root = system * (1.0 / norm)
        half = 0.5 * (diagonal - root)
        system_ref[i] = root
        inverse_ref[i] = diagonal + half
        change.append(split(half))

    for step in range(NS_ITERS):
        if step:
            change = []
            for i in range(LIVE):
                product = dot3(split(inverse_ref[i]), split(system_ref[i]))
                change.append(split(0.5 * (diagonal - product)))
        for i in range(LIVE):
            if step:
                inverse = inverse_ref[i]
                inverse_ref[i] = inverse + dot3(change[i], split(inverse))
            if step < NS_ITERS - 1:
                root = system_ref[i]
                system_ref[i] = root + dot3(split(root), change[i])

    first = pl.multiple_of(rank * PITCH, 8)
    last = pl.multiple_of(ranks * PITCH + rank // 2 * (2 * rest), 8)
    odd = lax.rem(rank, 2) == 1
    ones = jnp.ones((1, side), F32)
    inverses = [split(inverse_ref[i]) for i in range(LIVE)]
    half_way = [
        dot3(split(jnp.broadcast_to(pull[i], (8, side))), inverses[i]) for i in range(LIVE)
    ]
    mean_weights = [dot3(split(half_way[i]), inverses[i])[0:1, :] for i in range(LIVE)]
    for i in range(LIVE):
        mean_weight = mean_weights[i] * (1.0 / frobenius[i])
        ends = inverse_ref[i, pl.ds(last, 2 * rest), :]
        ends = jnp.where(odd, ends[rest:], ends[:rest])
        own = jnp.concatenate([inverse_ref[i, pl.ds(first, PITCH), :], ends], axis=0)
        transform = (math.sqrt(side - 1) * lax.rsqrt(frobenius[i])) * own + mean_weight
        transform = transform.astype(BF16).astype(F32)
        keep_share = 1.0 - jnp.sum(transform, axis=1, keepdims=True)
        weights = padded_to(jnp.concatenate([transform, ones], axis=0), 2 * PITCH).astype(BF16)
        state = [x for c in range(0, pieces, 2) for x in all_members((tiles + i * pieces + c) // 2)]
        for c in range(pieces):
            blended = dot(weights, state[c])
            mean_state = blended[members : members + 1, :] / side
            analysis = blended[:members] + keep_share * mean_state
            rows_ref[c, pl.ds(i, members, stride=PITCH), :] = jnp.where(i < live_count, analysis, 0.0)
    for i in range(LIVE, capacity):
        for c in range(pieces):
            rows_ref[c, pl.ds(i, members, stride=PITCH), :] = jnp.zeros((members, obs_slots), F32)
    for m in range(members):
        for c in range(pieces):
            span = slice(c * obs_slots, (c + 1) * obs_slots)
            out_ref[m, :, span] = rows_ref[c, m * PITCH : m * PITCH + capacity, :].astype(BF16)


def shards(
    background, obs_ens, innovation, precision, loc_weight,
    old_split, new_split, obs_count, halo_tiles, region_list,
):
    capacity, members, width = background.shape
    obs_slots = obs_ens.shape[2]
    devices = lax.axis_size("tile")
    ranks = lax.axis_size("mem")
    pieces = width // obs_slots
    tiles = LIVE + HPEER * HCAP
    smem = pl.BlockSpec(memory_space=SMEM)
    vmem = pl.BlockSpec(memory_space=VMEM)
    hbm = pl.BlockSpec(memory_space=pltpu.HBM)

    def params(mebibytes):
        return pltpu.CompilerParams(vmem_limit_bytes=mebibytes << 20)

    def tile_blocks(*leading):
        return jax.ShapeDtypeStruct((*leading, PADDED, obs_slots), BF16)

    background, obs_ens = background.transpose(1, 0, 2), obs_ens.transpose(1, 0, 2)
    halo_tiles, region_list, loc_weight = halo_tiles.T, region_list.T, loc_weight.T

    own, own_pulled, block, *swaps = pl.pallas_call(
        pack_kernel,
        out_shape=(
            tile_blocks(LIVE),
            jax.ShapeDtypeStruct((PITCH, obs_slots), F32),
            tile_blocks(BLOCK, HCAP + MOVE * pieces),
            tile_blocks(HCAP),
            tile_blocks(HCAP),
            tile_blocks(HCAP + MOVE * pieces),
        ),
        in_specs=[smem] * 4 + [vmem] * 4,
        out_specs=[vmem] * 6,
        scratch_shapes=[
            VMEM((members * PITCH, obs_slots), F32),
            VMEM((pieces, members * PITCH, obs_slots), F32),
        ],
        compiler_params=params(56),
    )(obs_count, old_split, new_split, halo_tiles, obs_ens, innovation, precision, background)

    groups = [list(range(b, b + BLOCK)) for b in range(0, devices, BLOCK)]
    block = lax.all_to_all(block, "tile", 0, 0, axis_index_groups=groups, tiled=True)
    arrived = []
    for swap, value in zip(SWAPS, swaps):
        pairs = [(d, d + swap[d % BLOCK]) for d in range(devices)]
        pairs = [(d, e) for d, e in pairs if 0 <= e < devices]
        arrived.append(lax.ppermute(value, "tile", pairs))

    table_shape = (ranks, (tiles + LIVE * pieces) // 2, 2 * members, obs_slots)
    table = pl.pallas_call(
        own_table_kernel,
        out_shape=jax.ShapeDtypeStruct(table_shape, BF16),
        in_specs=[smem] * 2 + [vmem] * 2,
        out_specs=pl.BlockSpec(memory_space=pl.ANY),
        scratch_shapes=[
            VMEM(table_shape[1:], BF16),
            VMEM((pieces, members * PITCH, obs_slots), F32),
            pltpu.SemaphoreType.DMA((ranks,)),
        ],
        compiler_params=params(56),
        cost_estimate=COST,
    )(old_split, new_split, own, background)
    table, halo_pulled = pl.pallas_call(
        table_kernel,
        out_shape=(
            jax.ShapeDtypeStruct(table_shape, BF16),
            jax.ShapeDtypeStruct((PITCH, obs_slots), F32),
        ),
        in_specs=[smem] * 3 + [pl.BlockSpec(memory_space=pl.ANY)] + [vmem] * 4,
        out_specs=(pl.BlockSpec(memory_space=pl.ANY), vmem),
        input_output_aliases={3: 0},
        scratch_shapes=[
            VMEM((HPEER * HCAP // 2, 2 * members, obs_slots), BF16),
            VMEM((2 * MOVE, pieces // 2, 2 * members, obs_slots), BF16),
            pltpu.SemaphoreType.DMA((ranks,)),
            pltpu.SemaphoreType.DMA((2 * MOVE, ranks)),
        ],
        compiler_params=params(16),
    )(old_split, new_split, halo_tiles, table, block, *arrived)
    table = lax.all_to_all(table, "mem", 0, 0, tiled=True)

    side = ranks * members
    analysis = pl.pallas_call(
        analysis_kernel,
        out_shape=jax.ShapeDtypeStruct((members, capacity, width), BF16),
        in_specs=[smem] * 3 + [vmem] * 3,
        out_specs=vmem,
        scratch_shapes=[
            VMEM((tiles, side + 8, side), F32),
            VMEM((LIVE, side, side), F32),
            VMEM((LIVE, side, side), F32),
            VMEM((pieces, members * PITCH, obs_slots), F32),
        ],
        compiler_params=params(28),
    )(region_list, loc_weight, new_split, own_pulled, halo_pulled, table)
    return analysis.transpose(1, 0, 2)


def solution(mesh):
    in_specs = (
        P("tile", "mem", None),
        P("tile", "mem", None),
        P("tile", None),
        P("tile", None),
        P("tile", None),
        P(),
        P(),
        P("tile"),
        P(),
        P("tile", None),
    )
    out_specs = P("tile", "mem", None)
    return jax.shard_map(shards, mesh=mesh, in_specs=in_specs, out_specs=out_specs, check_vma=False)
```

```python
import functools
import math

import jax
import jax.numpy as jnp
from jax import lax
from jax.experimental import pallas as pl
from jax.experimental.pallas import tpu as pltpu
from jax.sharding import PartitionSpec as P

MOVE = 2
REACH = 3
HPEER = 3
HCAP = 4
NS_ITERS = 6
LIVE = 10
BLOCK = 4
PADDED = 24
INFLATION = 1.1
COST = pl.CostEstimate(flops=1 << 20, bytes_accessed=4 << 20, transcendentals=0)
PITCH = 16

SWAPS = ((-3, 3, -3, 3), (-2, -2, 2, 2), (-1, -3, 3, 1))

SMEM = pltpu.SMEM
VMEM = pltpu.VMEM
F32 = jnp.float32
BF16 = jnp.bfloat16


def chosen(place, values):
    result = values[0]
    for k in range(1, len(values)):
        result = jnp.where(place == k, values[k], result)
    return result


def padded_to(x, rows):
    return jnp.concatenate([x, jnp.zeros((rows - x.shape[0], x.shape[1]), x.dtype)], axis=0)


def paired(x, y):
    x, y = x.astype(F32), y.astype(F32)
    parts = [x[:PITCH], y[:PITCH], x[PITCH:], y[PITCH:]]
    return jnp.concatenate(parts, axis=0).astype(BF16)


def pack_kernel(
    count_ref, old_ref, new_ref, halo_ref,
    obs_ref, innovation_ref, precision_ref, background_ref,
    own_ref, pulled_ref, block_ref, *refs,
):
    swap_refs, (obs_rows, state_rows) = refs[:-2], refs[-2:]
    devices = new_ref.shape[0] - 1
    me = lax.axis_index("tile")
    place = lax.rem(me, BLOCK)
    new_start, new_end = new_ref[me], new_ref[me + 1]
    members, capacity, obs_slots = obs_ref.shape
    pieces = background_ref.shape[2] // obs_slots

    lane = lax.broadcasted_iota(jnp.int32, (1, obs_slots), 1)
    live = [(lane < count_ref[i]).astype(F32) for i in range(capacity)]
    root = jnp.sqrt(precision_ref[...] * jnp.concatenate(live, axis=0))
    pulled = root * innovation_ref[...]
    for m in range(members):
        obs_rows[m * PITCH : m * PITCH + capacity, :] = obs_ref[m].astype(F32) * root
        for c in range(pieces):
            span = slice(c * obs_slots, (c + 1) * obs_slots)
            state_rows[c, m * PITCH : m * PITCH + capacity, :] = background_ref[m, :, span].astype(F32)
    pulled_ref[...] = padded_to(pulled, PITCH).astype(BF16).astype(F32)
    for i in range(LIVE):
        scaled = obs_rows[pl.ds(i, members, stride=PITCH), :]
        own_ref[i] = padded_to(jnp.concatenate([scaled, pulled[i : i + 1, :]], axis=0), PADDED).astype(BF16)

    def pack(reader, put):
        reader = jnp.clip(reader, 0, devices - 1)
        group = 0
        for g in range(1, HPEER):
            first = halo_ref[g * HCAP, reader]
            group = jnp.where((first >= new_start) & (first < new_end), g, group)
        for k in range(HCAP):
            row = jnp.clip(halo_ref[group * HCAP + k, reader] - new_start, 0, LIVE - 1)
            put(k, own_ref[row])

    for j in range(BLOCK):
        def put(k, value, j=j):
            block_ref[j, k] = value
        pack(me - place + j, put)
    for swap, swap_ref in zip(SWAPS, swap_refs):
        def put(k, value, swap_ref=swap_ref):
            swap_ref[k] = value
        pack(me + chosen(place, swap), put)

    old_count = old_ref[me + 1] - old_ref[me]
    for first, inside, slot in (
        (old_count - MOVE, place < BLOCK - 1, place + 1),
        (0, place > 0, place - 1),
    ):
        for t in range(MOVE):
            for c in range(pieces):
                piece = state_rows[c, pl.ds(first + t, members, stride=PITCH), :]
                piece = padded_to(piece, PADDED).astype(BF16)
                at = HCAP + t * pieces + c

                @pl.when(inside)
                def _():
                    block_ref[slot, at] = piece

                @pl.when(jnp.logical_not(inside))
                def _():
                    swap_refs[-1][at] = piece


def own_table_kernel(
    old_ref, new_ref, own_ref, background_ref, table_ref, state_rows
):
    me = lax.axis_index("tile")
    old_start, old_end, new_start = old_ref[me], old_ref[me + 1], new_ref[me]
    members, capacity, width = background_ref.shape
    obs_slots = own_ref.shape[2]
    pieces = width // obs_slots
    for m in range(members):
        for c in range(pieces):
            span = slice(c * obs_slots, (c + 1) * obs_slots)
            state_rows[c, m * PITCH : m * PITCH + capacity, :] = background_ref[m, :, span].astype(F32)
    for i in range(0, LIVE, 2):
        table_ref[i // 2] = paired(own_ref[i][:members], own_ref[i + 1][:members])
    for i in range(LIVE):
        at = jnp.clip(new_start + i - old_start, 0, capacity - 1)
        rows = [state_rows[c, pl.ds(at, members, stride=PITCH), :] for c in range(pieces)]
        for c in range(0, pieces, 2):
            table_ref[(LIVE + HPEER * HCAP + i * pieces + c) // 2] = paired(rows[c], rows[c + 1])


def table_kernel(old_ref, new_ref, halo_ref, stays_ref, block_ref, *refs):
    swap_refs, (out_ref, pulled_ref, table_ref, fetch_sem, sems) = refs[:-5], refs[-5:]
    fetch = pltpu.make_async_copy(stays_ref, table_ref, fetch_sem)
    fetch.start()
    devices = new_ref.shape[0] - 1
    me = lax.axis_index("tile")
    place = lax.rem(me, BLOCK)
    base = me - place
    old_start, old_end = old_ref[me], old_ref[me + 1]
    new_start, new_end = new_ref[me], new_ref[me + 1]
    ranks, _, pair_rows, _ = out_ref.shape
    members = pair_rows // 2
    pieces = (block_ref.shape[1] - HCAP) // MOVE
    pulled_ref[...] = jnp.zeros(pulled_ref.shape, F32)
    fetch.wait()

    moves = []
    for j in range(MOVE):
        tile = new_start + j
        index = jnp.clip(tile - old_start + MOVE, 0, MOVE - 1)
        moves.append((tile < old_start, j, index, place > 0, place - 1))
    for j in range(MOVE):
        tile = old_end + j
        slot = jnp.clip(tile - new_start, 0, LIVE - 1)
        moves.append((tile < new_end, slot, j, place < BLOCK - 1, place + 1))
    for comes, slot, index, inside, source in moves:
        begin = HCAP + index * pieces
        source = jnp.clip(source, 0, BLOCK - 1)
        at = (LIVE + HPEER * HCAP + slot * pieces) // 2

        def put(read, at=at):
            for c in range(0, pieces, 2):
                table_ref[at + c // 2] = paired(read(c)[:members], read(c + 1)[:members])

        @pl.when(comes & inside)
        def _():
            put(lambda c: block_ref[source, begin + c])

        @pl.when(comes & jnp.logical_not(inside))
        def _():
            put(lambda c: swap_refs[-1][begin + c])

    for g in range(HPEER):
        first = halo_ref[g * HCAP, me]
        peer = me - REACH
        for o in range(1 - REACH, REACH + 1):
            bound = new_ref[jnp.clip(me + o, 0, devices)]
            peer = peer + (bound <= first).astype(jnp.int32)

        def put(read, g=g):
            for k in range(HCAP):
                at = g * HCAP + k
                pulled_ref[at : at + 1, :] = read(k).astype(F32)[members : members + 1]
            for k in range(0, HCAP, 2):
                table_ref[(LIVE + g * HCAP + k) // 2] = paired(read(k)[:members], read(k + 1)[:members])

        @pl.when((peer >= base) & (peer < base + BLOCK))
        def _():
            slot = jnp.clip(peer - base, 0, BLOCK - 1)
            put(lambda k: block_ref[slot, k])

        for swap, swap_ref in zip(SWAPS, swap_refs):
            @pl.when(peer == me + chosen(place, swap))
            def _():
                put(lambda k: swap_ref[k])

    copies = [
        pltpu.make_async_copy(table_ref, out_ref.at[r], sems.at[r]) for r in range(ranks)
    ]
    for copy in copies:
        copy.start()
    for copy in copies:
        copy.wait()


def split(x):
    high = x.astype(BF16)
    return high, (x - high.astype(F32)).astype(BF16)


def dot(a, b):
    return jnp.dot(a, b, preferred_element_type=F32)


def dot3(a, b):
    return dot(a[0], b[0]) + (dot(a[0], b[1]) + dot(a[1], b[0]))


def analysis_kernel(
    region_ref, weight_ref, new_ref, own_pulled_ref, halo_pulled_ref, table_ref, out_ref,
    gram_ref, system_ref, inverse_ref, rows_ref,
):
    me = lax.axis_index("tile")
    rank = lax.axis_index("mem")
    ranks, tiles = table_ref.shape[0], LIVE + HPEER * HCAP
    members, capacity, width = out_ref.shape
    obs_slots = table_ref.shape[3]
    pieces = width // obs_slots
    ensemble = ranks * members
    side = ensemble + PITCH
    live_count = new_ref[me + 1] - new_ref[me]

    row = lax.broadcasted_iota(jnp.int32, (side, side), 0)
    column = lax.broadcasted_iota(jnp.int32, (side, side), 1)
    diagonal = (row == column).astype(F32)
    real = (row < ensemble) & (column < ensemble)
    shift = jnp.where(real, diagonal * ((ensemble - 1) / INFLATION), 0.0)
    real_lane = lax.broadcasted_iota(jnp.int32, (1, side), 1) < ensemble

    rest = members - PITCH

    upper = lax.broadcasted_iota(jnp.int32, (2 * rest, obs_slots), 0) < rest

    def all_members(pair):
        rows = [table_ref[r, pair].astype(F32) for r in range(ranks)]
        ends = [x[2 * PITCH :] for x in rows]
        turned = [pltpu.roll(x, rest, 0) for x in ends]
        blocks = []
        for k in range(2):
            parts = [x[k * PITCH : (k + 1) * PITCH] for x in rows]
            for r in range(0, ranks, 2):
                above = turned[r] if k else ends[r]
                below = ends[r + 1] if k else turned[r + 1]
                parts.append(jnp.where(upper, above, below))
            blocks.append(jnp.concatenate(parts, axis=0).astype(BF16))
        return blocks

    for t in range(0, tiles, 2):
        for k, block in enumerate(all_members(t // 2)):
            at = t + k
            pulled_ref, where = (own_pulled_ref, at) if at < LIVE else (halo_pulled_ref, at - LIVE)
            pulled = padded_to(pulled_ref[where : where + 1, :], PITCH).astype(BF16)
            block = jnp.concatenate([block, pulled], axis=0)
            gram_ref[at] = lax.dot_general(
                block, block, (((1,), (1,)), ((), ())), preferred_element_type=F32
            )

    frobenius, pull, change = [], [], []
    for i in range(LIVE):
        total = gram_ref[i]
        for e in range(region_ref.shape[0]):
            r = region_ref[e, i]
            at = jnp.where(r < capacity, jnp.minimum(r, LIVE - 1), r - capacity + LIVE)
            total = total + weight_ref[e, i] * gram_ref[at]
        pull.append(jnp.where(real_lane, total[ensemble : ensemble + 1, :], 0.0))
        system = jnp.where(real, total, 0.0) + shift
        squared = jnp.sum(jnp.sum(system * system, axis=0, keepdims=True), axis=1, keepdims=True)
        norm = jnp.sqrt(squared)
        frobenius.append(norm)
        root = system * (1.0 / norm)
        half = 0.5 * (diagonal - root)
        system_ref[i] = root
        inverse_ref[i] = diagonal + half
        change.append(split(half))

    for step in range(NS_ITERS):
        if step:
            change = []
            for i in range(LIVE):
                product = dot3(split(inverse_ref[i]), split(system_ref[i]))
                change.append(split(0.5 * (diagonal - product)))
        for i in range(LIVE):
            if step:
                inverse = inverse_ref[i]
                inverse_ref[i] = inverse + dot3(change[i], split(inverse))
            if step < NS_ITERS - 1:
                root = system_ref[i]
                system_ref[i] = root + dot3(split(root), change[i])

    first = pl.multiple_of(rank * PITCH, 8)
    last = pl.multiple_of(ranks * PITCH + rank // 2 * (2 * rest), 8)
    odd = lax.rem(rank, 2) == 1
    ones = jnp.ones((1, ensemble), F32)
    inverses = [split(inverse_ref[i]) for i in range(LIVE)]
    half_way = [
        dot3(split(jnp.broadcast_to(pull[i], (8, side))), inverses[i]) for i in range(LIVE)
    ]
    mean_weights = [dot3(split(half_way[i]), inverses[i])[0:1, :] for i in range(LIVE)]
    for i in range(LIVE):
        mean_weight = mean_weights[i] * (1.0 / frobenius[i])
        ends = inverse_ref[i, pl.ds(last, 2 * rest), :]
        ends = jnp.where(odd, ends[rest:], ends[:rest])
        own = jnp.concatenate([inverse_ref[i, pl.ds(first, PITCH), :], ends], axis=0)
        transform = (math.sqrt(ensemble - 1) * lax.rsqrt(frobenius[i])) * own + mean_weight
        transform = transform[:, :ensemble]
        transform = transform.astype(BF16).astype(F32)
        keep_share = 1.0 - jnp.sum(transform, axis=1, keepdims=True)
        weights = padded_to(jnp.concatenate([transform, ones], axis=0), 2 * PITCH).astype(BF16)
        state = [x for c in range(0, pieces, 2) for x in all_members((tiles + i * pieces + c) // 2)]
        for c in range(pieces):
            blended = dot(weights, state[c])
            mean_state = blended[members : members + 1, :] / ensemble
            analysis = blended[:members] + keep_share * mean_state
            rows_ref[c, pl.ds(i, members, stride=PITCH), :] = jnp.where(i < live_count, analysis, 0.0)
    for i in range(LIVE, capacity):
        for c in range(pieces):
            rows_ref[c, pl.ds(i, members, stride=PITCH), :] = jnp.zeros((members, obs_slots), F32)
    for m in range(members):
        for c in range(pieces):
            span = slice(c * obs_slots, (c + 1) * obs_slots)
            out_ref[m, :, span] = rows_ref[c, m * PITCH : m * PITCH + capacity, :].astype(BF16)


def shards(
    background, obs_ens, innovation, precision, loc_weight,
    old_split, new_split, obs_count, halo_tiles, region_list,
):
    capacity, members, width = background.shape
    obs_slots = obs_ens.shape[2]
    devices = lax.axis_size("tile")
    ranks = lax.axis_size("mem")
    pieces = width // obs_slots
    tiles = LIVE + HPEER * HCAP
    smem = pl.BlockSpec(memory_space=SMEM)
    vmem = pl.BlockSpec(memory_space=VMEM)
    hbm = pl.BlockSpec(memory_space=pltpu.HBM)

    def params(mebibytes):
        return pltpu.CompilerParams(vmem_limit_bytes=mebibytes << 20)

    def tile_blocks(*leading):
        return jax.ShapeDtypeStruct((*leading, PADDED, obs_slots), BF16)

    background, obs_ens = background.transpose(1, 0, 2), obs_ens.transpose(1, 0, 2)
    halo_tiles, region_list, loc_weight = halo_tiles.T, region_list.T, loc_weight.T

    own, own_pulled, block, *swaps = pl.pallas_call(
        pack_kernel,
        out_shape=(
            tile_blocks(LIVE),
            jax.ShapeDtypeStruct((PITCH, obs_slots), F32),
            tile_blocks(BLOCK, HCAP + MOVE * pieces),
            tile_blocks(HCAP),
            tile_blocks(HCAP),
            tile_blocks(HCAP + MOVE * pieces),
        ),
        in_specs=[smem] * 4 + [vmem] * 4,
        out_specs=[vmem] * 6,
        scratch_shapes=[
            VMEM((members * PITCH, obs_slots), F32),
            VMEM((pieces, members * PITCH, obs_slots), F32),
        ],
        compiler_params=params(56),
    )(obs_count, old_split, new_split, halo_tiles, obs_ens, innovation, precision, background)

    groups = [list(range(b, b + BLOCK)) for b in range(0, devices, BLOCK)]
    block = lax.all_to_all(block, "tile", 0, 0, axis_index_groups=groups, tiled=True)
    arrived = []
    for swap, value in zip(SWAPS, swaps):
        pairs = [(d, d + swap[d % BLOCK]) for d in range(devices)]
        pairs = [(d, e) for d, e in pairs if 0 <= e < devices]
        arrived.append(lax.ppermute(value, "tile", pairs))

    table_shape = ((tiles + LIVE * pieces) // 2, 2 * members, obs_slots)
    stays = pl.pallas_call(
        own_table_kernel,
        out_shape=jax.ShapeDtypeStruct(table_shape, BF16),
        in_specs=[smem] * 2 + [vmem] * 2,
        out_specs=vmem,
        scratch_shapes=[VMEM((pieces, members * PITCH, obs_slots), F32)],
        compiler_params=params(56),
        cost_estimate=COST,
    )(old_split, new_split, own, background)
    table, halo_pulled = pl.pallas_call(
        table_kernel,
        out_shape=(
            jax.ShapeDtypeStruct((ranks, *table_shape), BF16),
            jax.ShapeDtypeStruct((PITCH, obs_slots), F32),
        ),
        in_specs=[smem] * 3 + [pl.BlockSpec(memory_space=pl.ANY)] + [vmem] * 4,
        out_specs=(pl.BlockSpec(memory_space=pl.ANY), vmem),
        scratch_shapes=[
            VMEM(table_shape, BF16),
            pltpu.SemaphoreType.DMA,
            pltpu.SemaphoreType.DMA((ranks,)),
        ],
        compiler_params=params(16),
    )(old_split, new_split, halo_tiles, stays, block, *arrived)
    table = lax.all_to_all(table, "mem", 0, 0, tiled=True)

    side = ranks * members + PITCH
    analysis = pl.pallas_call(
        analysis_kernel,
        out_shape=jax.ShapeDtypeStruct((members, capacity, width), BF16),
        in_specs=[smem] * 3 + [vmem] * 3,
        out_specs=vmem,
        scratch_shapes=[
            VMEM((tiles, side, side), F32),
            VMEM((LIVE, side, side), F32),
            VMEM((LIVE, side, side), F32),
            VMEM((pieces, members * PITCH, obs_slots), F32),
        ],
        compiler_params=params(28),
    )(region_list, loc_weight, new_split, own_pulled, halo_pulled, table)
    return analysis.transpose(1, 0, 2)


def solution(mesh):
    in_specs = (
        P("tile", "mem", None),
        P("tile", "mem", None),
        P("tile", None),
        P("tile", None),
        P("tile", None),
        P(),
        P(),
        P("tile"),
        P(),
        P("tile", None),
    )
    out_specs = P("tile", "mem", None)
    return jax.shard_map(shards, mesh=mesh, in_specs=in_specs, out_specs=out_specs, check_vma=False)
```

```python
import functools
import math

import jax
import jax.numpy as jnp
from jax import lax
from jax.experimental import pallas as pl
from jax.experimental.pallas import tpu as pltpu
from jax.sharding import PartitionSpec as P

MOVE = 2
REACH = 3
HPEER = 3
HCAP = 4
NS_ITERS = 6
LIVE = 10
BLOCK = 4
PADDED = 24
INFLATION = 1.1
COST = pl.CostEstimate(flops=1 << 20, bytes_accessed=4 << 20, transcendentals=0)
ROOM = 40
PITCH = 16

SWAPS = ((-3, 3, -3, 3), (-2, -2, 2, 2), (-1, -3, 3, 1))

SMEM = pltpu.SMEM
VMEM = pltpu.VMEM
F32 = jnp.float32
BF16 = jnp.bfloat16


def chosen(place, values):
    result = values[0]
    for k in range(1, len(values)):
        result = jnp.where(place == k, values[k], result)
    return result


def padded_to(x, rows):
    return jnp.concatenate([x, jnp.zeros((rows - x.shape[0], x.shape[1]), x.dtype)], axis=0)


def paired(x, y):
    x, y = x.astype(F32), y.astype(F32)
    parts = [x[:PITCH], y[:PITCH], x[PITCH:], y[PITCH:]]
    return jnp.concatenate(parts, axis=0).astype(BF16)


def pack_kernel(
    count_ref, old_ref, new_ref, halo_ref,
    obs_ref, innovation_ref, precision_ref, background_ref,
    own_ref, pulled_ref, block_ref, *refs,
):
    swap_refs, (obs_rows, state_rows) = refs[:-2], refs[-2:]
    devices = new_ref.shape[0] - 1
    me = lax.axis_index("tile")
    place = lax.rem(me, BLOCK)
    new_start, new_end = new_ref[me], new_ref[me + 1]
    members, capacity, obs_slots = obs_ref.shape
    pieces = background_ref.shape[2] // obs_slots

    lane = lax.broadcasted_iota(jnp.int32, (1, obs_slots), 1)
    live = [(lane < count_ref[i]).astype(F32) for i in range(capacity)]
    root = jnp.sqrt(precision_ref[...] * jnp.concatenate(live, axis=0))
    pulled = root * innovation_ref[...]
    for m in range(members):
        obs_rows[m * PITCH : m * PITCH + capacity, :] = obs_ref[m].astype(F32) * root
        for c in range(pieces):
            span = slice(c * obs_slots, (c + 1) * obs_slots)
            state_rows[c, m * PITCH : m * PITCH + capacity, :] = background_ref[m, :, span].astype(F32)
    pulled_ref[...] = padded_to(pulled, PITCH).astype(BF16).astype(F32)
    for i in range(LIVE):
        scaled = obs_rows[pl.ds(i, members, stride=PITCH), :]
        own_ref[i] = padded_to(jnp.concatenate([scaled, pulled[i : i + 1, :]], axis=0), PADDED).astype(BF16)

    def pack(reader, put):
        reader = jnp.clip(reader, 0, devices - 1)
        group = 0
        for g in range(1, HPEER):
            first = halo_ref[g * HCAP, reader]
            group = jnp.where((first >= new_start) & (first < new_end), g, group)
        for k in range(HCAP):
            row = jnp.clip(halo_ref[group * HCAP + k, reader] - new_start, 0, LIVE - 1)
            put(k, own_ref[row])

    for j in range(BLOCK):
        def put(k, value, j=j):
            block_ref[j, k] = value
        pack(me - place + j, put)
    for swap, swap_ref in zip(SWAPS, swap_refs):
        def put(k, value, swap_ref=swap_ref):
            swap_ref[k] = value
        pack(me + chosen(place, swap), put)

    old_count = old_ref[me + 1] - old_ref[me]
    for first, inside, slot in (
        (old_count - MOVE, place < BLOCK - 1, place + 1),
        (0, place > 0, place - 1),
    ):
        for t in range(MOVE):
            for c in range(pieces):
                piece = state_rows[c, pl.ds(first + t, members, stride=PITCH), :]
                piece = padded_to(piece, PADDED).astype(BF16)
                at = HCAP + t * pieces + c

                @pl.when(inside)
                def _():
                    block_ref[slot, at] = piece

                @pl.when(jnp.logical_not(inside))
                def _():
                    swap_refs[-1][at] = piece


def own_table_kernel(
    old_ref, new_ref, own_ref, background_ref, out_ref, table_ref, state_rows, sem
):
    me = lax.axis_index("tile")
    old_start, old_end, new_start = old_ref[me], old_ref[me + 1], new_ref[me]
    members, capacity, width = background_ref.shape
    obs_slots = own_ref.shape[2]
    pieces = width // obs_slots
    for m in range(members):
        for c in range(pieces):
            span = slice(c * obs_slots, (c + 1) * obs_slots)
            state_rows[c, m * PITCH : m * PITCH + capacity, :] = background_ref[m, :, span].astype(F32)
    for i in range(0, LIVE, 2):
        table_ref[i // 2] = paired(own_ref[i][:members], own_ref[i + 1][:members])
    for i in range(LIVE):
        at = jnp.clip(new_start + i - old_start, 0, capacity - 1)
        rows = [state_rows[c, pl.ds(at, members, stride=PITCH), :] for c in range(pieces)]
        for c in range(0, pieces, 2):
            table_ref[(LIVE + HPEER * HCAP + i * pieces + c) // 2] = paired(rows[c], rows[c + 1])
    copy = pltpu.make_async_copy(table_ref, out_ref.at[0], sem)
    copy.start()
    copy.wait()


def table_kernel(old_ref, new_ref, halo_ref, stays_ref, block_ref, *refs):
    swap_refs, (out_ref, pulled_ref, table_ref, fetch_sem, sems) = refs[:-5], refs[-5:]
    fetch = pltpu.make_async_copy(stays_ref.at[0], table_ref, fetch_sem)
    fetch.start()
    devices = new_ref.shape[0] - 1
    me = lax.axis_index("tile")
    place = lax.rem(me, BLOCK)
    base = me - place
    old_start, old_end = old_ref[me], old_ref[me + 1]
    new_start, new_end = new_ref[me], new_ref[me + 1]
    ranks, _, pair_rows, _ = out_ref.shape
    members = pair_rows // 2
    pieces = (block_ref.shape[1] - HCAP) // MOVE
    pulled_ref[...] = jnp.zeros(pulled_ref.shape, F32)
    fetch.wait()

    moves = []
    for j in range(MOVE):
        tile = new_start + j
        index = jnp.clip(tile - old_start + MOVE, 0, MOVE - 1)
        moves.append((tile < old_start, j, index, place > 0, place - 1))
    for j in range(MOVE):
        tile = old_end + j
        slot = jnp.clip(tile - new_start, 0, LIVE - 1)
        moves.append((tile < new_end, slot, j, place < BLOCK - 1, place + 1))
    for comes, slot, index, inside, source in moves:
        begin = HCAP + index * pieces
        source = jnp.clip(source, 0, BLOCK - 1)
        at = (LIVE + HPEER * HCAP + slot * pieces) // 2

        def put(read, at=at):
            for c in range(0, pieces, 2):
                table_ref[at + c // 2] = paired(read(c)[:members], read(c + 1)[:members])

        @pl.when(comes & inside)
        def _():
            put(lambda c: block_ref[source, begin + c])

        @pl.when(comes & jnp.logical_not(inside))
        def _():
            put(lambda c: swap_refs[-1][begin + c])

    for g in range(HPEER):
        first = halo_ref[g * HCAP, me]
        peer = me - REACH
        for o in range(1 - REACH, REACH + 1):
            bound = new_ref[jnp.clip(me + o, 0, devices)]
            peer = peer + (bound <= first).astype(jnp.int32)

        def put(read, g=g):
            for k in range(HCAP):
                at = g * HCAP + k
                pulled_ref[at : at + 1, :] = read(k).astype(F32)[members : members + 1]
            for k in range(0, HCAP, 2):
                table_ref[(LIVE + g * HCAP + k) // 2] = paired(read(k)[:members], read(k + 1)[:members])

        @pl.when((peer >= base) & (peer < base + BLOCK))
        def _():
            slot = jnp.clip(peer - base, 0, BLOCK - 1)
            put(lambda k: block_ref[slot, k])

        for swap, swap_ref in zip(SWAPS, swap_refs):
            @pl.when(peer == me + chosen(place, swap))
            def _():
                put(lambda k: swap_ref[k])

    copies = [
        pltpu.make_async_copy(table_ref, out_ref.at[r], sems.at[r]) for r in range(ranks)
    ]
    for copy in copies:
        copy.start()
    for copy in copies:
        copy.wait()


def split(x):
    high = x.astype(BF16)
    return high, (x - high.astype(F32)).astype(BF16)


def dot(a, b):
    return jnp.dot(a, b, preferred_element_type=F32)


def dot3(a, b):
    rows = a[0].shape[0]
    both = dot(jnp.concatenate(a, axis=0), b[0])
    return both[:rows] + (both[rows:] + dot(a[0], b[1]))


def analysis_kernel(
    region_ref, weight_ref, new_ref, own_pulled_ref, halo_pulled_ref, table_ref, out_ref,
    gram_ref, system_ref, inverse_ref, rows_ref,
):
    me = lax.axis_index("tile")
    rank = lax.axis_index("mem")
    ranks, tiles = table_ref.shape[0], LIVE + HPEER * HCAP
    members, capacity, width = out_ref.shape
    obs_slots = table_ref.shape[3]
    pieces = width // obs_slots
    ensemble = ranks * members
    side = ensemble + PITCH
    live_count = new_ref[me + 1] - new_ref[me]

    row = lax.broadcasted_iota(jnp.int32, (side, side), 0)
    column = lax.broadcasted_iota(jnp.int32, (side, side), 1)
    diagonal = (row == column).astype(F32)
    real = (row < ensemble) & (column < ensemble)
    shift = jnp.where(real, diagonal * ((ensemble - 1) / INFLATION), 0.0)
    real_lane = lax.broadcasted_iota(jnp.int32, (1, side), 1) < ensemble

    rest = members - PITCH

    upper = lax.broadcasted_iota(jnp.int32, (2 * rest, obs_slots), 0) < rest

    def all_members(pair):
        rows = [table_ref[r, pair].astype(F32) for r in range(ranks)]
        ends = [x[2 * PITCH :] for x in rows]
        turned = [pltpu.roll(x, rest, 0) for x in ends]
        blocks = []
        for k in range(2):
            parts = [x[k * PITCH : (k + 1) * PITCH] for x in rows]
            for r in range(0, ranks, 2):
                above = turned[r] if k else ends[r]
                below = ends[r + 1] if k else turned[r + 1]
                parts.append(jnp.where(upper, above, below))
            blocks.append(jnp.concatenate(parts, axis=0).astype(BF16))
        return blocks

    for t in range(0, tiles, 2):
        for k, block in enumerate(all_members(t // 2)):
            at = t + k
            pulled_ref, where = (own_pulled_ref, at) if at < LIVE else (halo_pulled_ref, at - LIVE)
            pulled = padded_to(pulled_ref[where : where + 1, :], PITCH).astype(BF16)
            block = jnp.concatenate([block, pulled], axis=0)
            gram_ref[at] = lax.dot_general(
                block, block, (((1,), (1,)), ((), ())), preferred_element_type=F32
            )

    frobenius, pull, change = [], [], []
    for i in range(LIVE):
        total = gram_ref[i]
        for e in range(region_ref.shape[0]):
            r = region_ref[e, i]
            at = jnp.where(r < capacity, jnp.minimum(r, LIVE - 1), r - capacity + LIVE)
            total = total + weight_ref[e, i] * gram_ref[at]
        pull.append(jnp.where(real_lane, total[ensemble : ensemble + 1, :], 0.0))
        system = jnp.where(real, total, 0.0) + shift
        squared = jnp.sum(jnp.sum(system * system, axis=0, keepdims=True), axis=1, keepdims=True)
        norm = jnp.sqrt(squared)
        frobenius.append(norm)
        root = system * (1.0 / norm)
        half = 0.5 * (diagonal - root)
        system_ref[i] = root
        inverse_ref[i] = diagonal + half
        change.append(split(half))

    for step in range(NS_ITERS):
        if step:
            change = []
            for i in range(LIVE):
                product = dot3(split(inverse_ref[i]), split(system_ref[i]))
                change.append(split(0.5 * (diagonal - product)))
        for i in range(LIVE):
            if step:
                inverse = inverse_ref[i]
                inverse_ref[i] = inverse + dot3(change[i], split(inverse))
            if step < NS_ITERS - 1:
                root = system_ref[i]
                system_ref[i] = root + dot3(split(root), change[i])

    first = pl.multiple_of(rank * PITCH, 8)
    last = pl.multiple_of(ranks * PITCH + rank // 2 * (2 * rest), 8)
    odd = lax.rem(rank, 2) == 1
    ones = jnp.ones((1, ensemble), F32)
    inverses = [split(inverse_ref[i]) for i in range(LIVE)]
    half_way = [
        dot3(split(jnp.broadcast_to(pull[i], (8, side))), inverses[i]) for i in range(LIVE)
    ]
    mean_weights = [dot3(split(half_way[i]), inverses[i])[0:1, :] for i in range(LIVE)]
    for i in range(LIVE):
        mean_weight = mean_weights[i] * (1.0 / frobenius[i])
        ends = inverse_ref[i, pl.ds(last, 2 * rest), :]
        ends = jnp.where(odd, ends[rest:], ends[:rest])
        own = jnp.concatenate([inverse_ref[i, pl.ds(first, PITCH), :], ends], axis=0)
        transform = (math.sqrt(ensemble - 1) * lax.rsqrt(frobenius[i])) * own + mean_weight
        transform = transform[:, :ensemble]
        transform = transform.astype(BF16).astype(F32)
        keep_share = 1.0 - jnp.sum(transform, axis=1, keepdims=True)
        weights = padded_to(jnp.concatenate([transform, ones], axis=0), 2 * PITCH).astype(BF16)
        state = [x for c in range(0, pieces, 2) for x in all_members((tiles + i * pieces + c) // 2)]
        for c in range(pieces):
            blended = dot(weights, state[c])
            mean_state = blended[members : members + 1, :] / ensemble
            analysis = blended[:members] + keep_share * mean_state
            rows_ref[c, pl.ds(i, members, stride=PITCH), :] = jnp.where(i < live_count, analysis, 0.0)
    for i in range(LIVE, capacity):
        for c in range(pieces):
            rows_ref[c, pl.ds(i, members, stride=PITCH), :] = jnp.zeros((members, obs_slots), F32)
    for m in range(members):
        for c in range(pieces):
            span = slice(c * obs_slots, (c + 1) * obs_slots)
            out_ref[m, :, span] = rows_ref[c, m * PITCH : m * PITCH + capacity, :].astype(BF16)


def shards(
    background, obs_ens, innovation, precision, loc_weight,
    old_split, new_split, obs_count, halo_tiles, region_list,
):
    capacity, members, width = background.shape
    obs_slots = obs_ens.shape[2]
    devices = lax.axis_size("tile")
    ranks = lax.axis_size("mem")
    pieces = width // obs_slots
    tiles = LIVE + HPEER * HCAP
    smem = pl.BlockSpec(memory_space=SMEM)
    vmem = pl.BlockSpec(memory_space=VMEM)
    hbm = pl.BlockSpec(memory_space=pltpu.HBM)

    def params(mebibytes):
        return pltpu.CompilerParams(vmem_limit_bytes=mebibytes << 20)

    def tile_blocks(*leading):
        return jax.ShapeDtypeStruct((*leading, PADDED, obs_slots), BF16)

    background, obs_ens = background.transpose(1, 0, 2), obs_ens.transpose(1, 0, 2)
    halo_tiles, region_list, loc_weight = halo_tiles.T, region_list.T, loc_weight.T

    own, own_pulled, block, *swaps = pl.pallas_call(
        pack_kernel,
        out_shape=(
            tile_blocks(LIVE),
            jax.ShapeDtypeStruct((PITCH, obs_slots), F32),
            tile_blocks(BLOCK, HCAP + MOVE * pieces),
            tile_blocks(HCAP),
            tile_blocks(HCAP),
            tile_blocks(HCAP + MOVE * pieces),
        ),
        in_specs=[smem] * 4 + [vmem] * 4,
        out_specs=[vmem] * 6,
        scratch_shapes=[
            VMEM((members * PITCH, obs_slots), F32),
            VMEM((pieces, members * PITCH, obs_slots), F32),
        ],
        compiler_params=params(56),
    )(obs_count, old_split, new_split, halo_tiles, obs_ens, innovation, precision, background)

    groups = [list(range(b, b + BLOCK)) for b in range(0, devices, BLOCK)]
    block = lax.all_to_all(block, "tile", 0, 0, axis_index_groups=groups, tiled=True)
    arrived = []
    for swap, value in zip(SWAPS, swaps):
        pairs = [(d, d + swap[d % BLOCK]) for d in range(devices)]
        pairs = [(d, e) for d, e in pairs if 0 <= e < devices]
        arrived.append(lax.ppermute(value, "tile", pairs))

    table_shape = ((tiles + LIVE * pieces) // 2, 2 * members, obs_slots)
    stays = pl.pallas_call(
        own_table_kernel,
        out_shape=jax.ShapeDtypeStruct((ROOM, *table_shape), BF16),
        in_specs=[smem] * 2 + [vmem] * 2,
        out_specs=pl.BlockSpec(memory_space=pl.ANY),
        scratch_shapes=[
            VMEM(table_shape, BF16),
            VMEM((pieces, members * PITCH, obs_slots), F32),
            pltpu.SemaphoreType.DMA,
        ],
        compiler_params=params(56),
        cost_estimate=COST,
    )(old_split, new_split, own, background)
    table, halo_pulled = pl.pallas_call(
        table_kernel,
        out_shape=(
            jax.ShapeDtypeStruct((ranks, *table_shape), BF16),
            jax.ShapeDtypeStruct((PITCH, obs_slots), F32),
        ),
        in_specs=[smem] * 3 + [pl.BlockSpec(memory_space=pl.ANY)] + [vmem] * 4,
        out_specs=(pl.BlockSpec(memory_space=pl.ANY), vmem),
        scratch_shapes=[
            VMEM(table_shape, BF16),
            pltpu.SemaphoreType.DMA,
            pltpu.SemaphoreType.DMA((ranks,)),
        ],
        compiler_params=params(50),
    )(old_split, new_split, halo_tiles, stays, block, *arrived)
    table = lax.all_to_all(table, "mem", 0, 0, tiled=True)

    side = ranks * members + PITCH
    analysis = pl.pallas_call(
        analysis_kernel,
        out_shape=jax.ShapeDtypeStruct((members, capacity, width), BF16),
        in_specs=[smem] * 3 + [vmem] * 3,
        out_specs=vmem,
        scratch_shapes=[
            VMEM((tiles, side, side), F32),
            VMEM((LIVE, side, side), F32),
            VMEM((LIVE, side, side), F32),
            VMEM((pieces, members * PITCH, obs_slots), F32),
        ],
        compiler_params=params(28),
    )(region_list, loc_weight, new_split, own_pulled, halo_pulled, table)
    return analysis.transpose(1, 0, 2)


def solution(mesh):
    in_specs = (
        P("tile", "mem", None),
        P("tile", "mem", None),
        P("tile", None),
        P("tile", None),
        P("tile", None),
        P(),
        P(),
        P("tile"),
        P(),
        P("tile", None),
    )
    out_specs = P("tile", "mem", None)
    return jax.shard_map(shards, mesh=mesh, in_specs=in_specs, out_specs=out_specs, check_vma=False)
```

```python
import functools
import math

import jax
import jax.numpy as jnp
from jax import lax
from jax.experimental import pallas as pl
from jax.experimental.pallas import tpu as pltpu
from jax.sharding import PartitionSpec as P

MOVE = 2
REACH = 3
HPEER = 3
HCAP = 4
NS_ITERS = 6
LIVE = 10
BLOCK = 4
PADDED = 24
INFLATION = 1.1
COST = pl.CostEstimate(flops=1 << 20, bytes_accessed=4 << 20, transcendentals=0)
ROOM = 40
PITCH = 16

SWAPS = ((-3, 3, -3, 3), (-2, -2, 2, 2), (-1, -3, 3, 1))

SMEM = pltpu.SMEM
VMEM = pltpu.VMEM
F32 = jnp.float32
BF16 = jnp.bfloat16


def chosen(place, values):
    result = values[0]
    for k in range(1, len(values)):
        result = jnp.where(place == k, values[k], result)
    return result


def padded_to(x, rows):
    return jnp.concatenate([x, jnp.zeros((rows - x.shape[0], x.shape[1]), x.dtype)], axis=0)


def paired(x, y):
    x, y = x.astype(F32), y.astype(F32)
    parts = [x[:PITCH], y[:PITCH], x[PITCH:], y[PITCH:]]
    return jnp.concatenate(parts, axis=0).astype(BF16)


def pack_kernel(
    count_ref, old_ref, new_ref, halo_ref,
    obs_ref, innovation_ref, precision_ref, background_ref,
    own_ref, pulled_ref, block_ref, *refs,
):
    swap_refs, (obs_rows, state_rows) = refs[:-2], refs[-2:]
    devices = new_ref.shape[0] - 1
    me = lax.axis_index("tile")
    place = lax.rem(me, BLOCK)
    new_start, new_end = new_ref[me], new_ref[me + 1]
    members, capacity, obs_slots = obs_ref.shape
    pieces = background_ref.shape[2] // obs_slots

    lane = lax.broadcasted_iota(jnp.int32, (1, obs_slots), 1)
    live = [(lane < count_ref[i]).astype(F32) for i in range(capacity)]
    root = jnp.sqrt(precision_ref[...] * jnp.concatenate(live, axis=0))
    pulled = root * innovation_ref[...]
    for m in range(members):
        obs_rows[m * PITCH : m * PITCH + capacity, :] = obs_ref[m].astype(F32) * root
        for c in range(pieces):
            span = slice(c * obs_slots, (c + 1) * obs_slots)
            state_rows[c, m * PITCH : m * PITCH + capacity, :] = background_ref[m, :, span].astype(F32)
    pulled_ref[...] = padded_to(pulled, PITCH).astype(BF16).astype(F32)
    for i in range(LIVE):
        scaled = obs_rows[pl.ds(i, members, stride=PITCH), :]
        own_ref[i] = padded_to(jnp.concatenate([scaled, pulled[i : i + 1, :]], axis=0), PADDED).astype(BF16)

    def pack(reader, put):
        reader = jnp.clip(reader, 0, devices - 1)
        group = 0
        for g in range(1, HPEER):
            first = halo_ref[g * HCAP, reader]
            group = jnp.where((first >= new_start) & (first < new_end), g, group)
        for k in range(HCAP):
            row = jnp.clip(halo_ref[group * HCAP + k, reader] - new_start, 0, LIVE - 1)
            put(k, own_ref[row])

    for j in range(BLOCK):
        def put(k, value, j=j):
            block_ref[j, k] = value
        pack(me - place + j, put)
    for swap, swap_ref in zip(SWAPS, swap_refs):
        def put(k, value, swap_ref=swap_ref):
            swap_ref[k] = value
        pack(me + chosen(place, swap), put)

    old_count = old_ref[me + 1] - old_ref[me]
    for first, inside, slot in (
        (old_count - MOVE, place < BLOCK - 1, place + 1),
        (0, place > 0, place - 1),
    ):
        for t in range(MOVE):
            for c in range(pieces):
                piece = state_rows[c, pl.ds(first + t, members, stride=PITCH), :]
                piece = padded_to(piece, PADDED).astype(BF16)
                at = HCAP + t * pieces + c

                @pl.when(inside)
                def _():
                    block_ref[slot, at] = piece

                @pl.when(jnp.logical_not(inside))
                def _():
                    swap_refs[-1][at] = piece


def own_table_kernel(
    old_ref, new_ref, own_ref, background_ref, out_ref, table_ref, state_rows, sem
):
    me = lax.axis_index("tile")
    old_start, old_end, new_start = old_ref[me], old_ref[me + 1], new_ref[me]
    members, capacity, width = background_ref.shape
    obs_slots = own_ref.shape[2]
    pieces = width // obs_slots
    for m in range(members):
        for c in range(pieces):
            span = slice(c * obs_slots, (c + 1) * obs_slots)
            state_rows[c, m * PITCH : m * PITCH + capacity, :] = background_ref[m, :, span].astype(F32)
    for i in range(0, LIVE, 2):
        table_ref[i // 2] = paired(own_ref[i][:members], own_ref[i + 1][:members])
    for i in range(LIVE):
        at = jnp.clip(new_start + i - old_start, 0, capacity - 1)
        rows = [state_rows[c, pl.ds(at, members, stride=PITCH), :] for c in range(pieces)]
        for c in range(0, pieces, 2):
            table_ref[(LIVE + HPEER * HCAP + i * pieces + c) // 2] = paired(rows[c], rows[c + 1])
    copy = pltpu.make_async_copy(table_ref, out_ref.at[0], sem)
    copy.start()
    copy.wait()


def table_kernel(old_ref, new_ref, halo_ref, stays_ref, block_ref, *refs):
    swap_refs, (out_ref, pulled_ref, table_ref, fetch_sem, sems) = refs[:-5], refs[-5:]
    fetch = pltpu.make_async_copy(stays_ref.at[0], table_ref, fetch_sem)
    fetch.start()
    devices = new_ref.shape[0] - 1
    me = lax.axis_index("tile")
    place = lax.rem(me, BLOCK)
    base = me - place
    old_start, old_end = old_ref[me], old_ref[me + 1]
    new_start, new_end = new_ref[me], new_ref[me + 1]
    ranks, _, pair_rows, _ = out_ref.shape
    members = pair_rows // 2
    pieces = (block_ref.shape[1] - HCAP) // MOVE
    pulled_ref[...] = jnp.zeros(pulled_ref.shape, F32)
    fetch.wait()

    moves = []
    for j in range(MOVE):
        tile = new_start + j
        index = jnp.clip(tile - old_start + MOVE, 0, MOVE - 1)
        moves.append((tile < old_start, j, index, place > 0, place - 1))
    for j in range(MOVE):
        tile = old_end + j
        slot = jnp.clip(tile - new_start, 0, LIVE - 1)
        moves.append((tile < new_end, slot, j, place < BLOCK - 1, place + 1))
    for comes, slot, index, inside, source in moves:
        begin = HCAP + index * pieces
        source = jnp.clip(source, 0, BLOCK - 1)
        at = (LIVE + HPEER * HCAP + slot * pieces) // 2

        def put(read, at=at):
            for c in range(0, pieces, 2):
                table_ref[at + c // 2] = paired(read(c)[:members], read(c + 1)[:members])

        @pl.when(comes & inside)
        def _():
            put(lambda c: block_ref[source, begin + c])

        @pl.when(comes & jnp.logical_not(inside))
        def _():
            put(lambda c: swap_refs[-1][begin + c])

    for g in range(HPEER):
        first = halo_ref[g * HCAP, me]
        peer = me - REACH
        for o in range(1 - REACH, REACH + 1):
            bound = new_ref[jnp.clip(me + o, 0, devices)]
            peer = peer + (bound <= first).astype(jnp.int32)

        def put(read, g=g):
            for k in range(HCAP):
                at = g * HCAP + k
                pulled_ref[at : at + 1, :] = read(k).astype(F32)[members : members + 1]
            for k in range(0, HCAP, 2):
                table_ref[(LIVE + g * HCAP + k) // 2] = paired(read(k)[:members], read(k + 1)[:members])

        @pl.when((peer >= base) & (peer < base + BLOCK))
        def _():
            slot = jnp.clip(peer - base, 0, BLOCK - 1)
            put(lambda k: block_ref[slot, k])

        for swap, swap_ref in zip(SWAPS, swap_refs):
            @pl.when(peer == me + chosen(place, swap))
            def _():
                put(lambda k: swap_ref[k])

    copies = [
        pltpu.make_async_copy(table_ref, out_ref.at[r], sems.at[r]) for r in range(ranks)
    ]
    for copy in copies:
        copy.start()
    for copy in copies:
        copy.wait()


def split(x):
    high = x.astype(BF16)
    return high, (x - high.astype(F32)).astype(BF16)


def dot(a, b):
    return jnp.dot(a, b, preferred_element_type=F32)


def dot3(a, b):
    rows = a[0].shape[0]
    both = dot(jnp.concatenate(a, axis=0), b[0])
    return both[:rows] + (both[rows:] + dot(a[0], b[1]))


def analysis_kernel(
    region_ref, weight_ref, new_ref, own_pulled_ref, halo_pulled_ref, table_ref, out_ref,
    gram_ref, system_ref, inverse_ref, rows_ref,
):
    me = lax.axis_index("tile")
    rank = lax.axis_index("mem")
    ranks, tiles = table_ref.shape[0], LIVE + HPEER * HCAP
    members, capacity, width = out_ref.shape
    obs_slots = table_ref.shape[3]
    pieces = width // obs_slots
    ensemble = ranks * members
    side = ensemble + PITCH
    live_count = new_ref[me + 1] - new_ref[me]

    row = lax.broadcasted_iota(jnp.int32, (side, side), 0)
    column = lax.broadcasted_iota(jnp.int32, (side, side), 1)
    diagonal = (row == column).astype(F32)
    real = (row < ensemble) & (column < ensemble)
    shift = jnp.where(real, diagonal * ((ensemble - 1) / INFLATION), 0.0)
    real_lane = lax.broadcasted_iota(jnp.int32, (1, side), 1) < ensemble

    rest = members - PITCH

    upper = lax.broadcasted_iota(jnp.int32, (2 * rest, obs_slots), 0) < rest

    def all_members(pair):
        rows = [table_ref[r, pair].astype(F32) for r in range(ranks)]
        ends = [x[2 * PITCH :] for x in rows]
        turned = [pltpu.roll(x, rest, 0) for x in ends]
        blocks = []
        for k in range(2):
            parts = [x[k * PITCH : (k + 1) * PITCH] for x in rows]
            for r in range(0, ranks, 2):
                above = turned[r] if k else ends[r]
                below = ends[r + 1] if k else turned[r + 1]
                parts.append(jnp.where(upper, above, below))
            blocks.append(jnp.concatenate(parts, axis=0).astype(BF16))
        return blocks

    for t in range(0, tiles, 2):
        for k, block in enumerate(all_members(t // 2)):
            at = t + k
            pulled_ref, where = (own_pulled_ref, at) if at < LIVE else (halo_pulled_ref, at - LIVE)
            pulled = padded_to(pulled_ref[where : where + 1, :], PITCH).astype(BF16)
            block = jnp.concatenate([block, pulled], axis=0)
            gram_ref[at] = lax.dot_general(
                block, block, (((1,), (1,)), ((), ())), preferred_element_type=F32
            )

    frobenius, pull, change = [], [], []
    for i in range(LIVE):
        total = gram_ref[i]
        for e in range(region_ref.shape[0]):
            r = region_ref[e, i]
            at = jnp.where(r < capacity, jnp.minimum(r, LIVE - 1), r - capacity + LIVE)
            total = total + weight_ref[e, i] * gram_ref[at]
        pull.append(jnp.where(real_lane, total[ensemble : ensemble + 1, :], 0.0))
        system = jnp.where(real, total, 0.0) + shift
        squared = jnp.sum(jnp.sum(system * system, axis=0, keepdims=True), axis=1, keepdims=True)
        norm = jnp.sqrt(squared)
        frobenius.append(norm)
        root = system * (1.0 / norm)
        half = 0.5 * (diagonal - root)
        system_ref[i] = root
        inverse_ref[i] = diagonal + half
        change.append(half.astype(BF16))

    for step in range(NS_ITERS):
        if step:
            change = []
            for i in range(LIVE):
                product = dot3(split(inverse_ref[i]), split(system_ref[i]))
                change.append((0.5 * (diagonal - product)).astype(BF16))
        for i in range(LIVE):
            if step:
                inverse = inverse_ref[i]
                inverse_ref[i] = inverse + dot(change[i], inverse.astype(BF16))
            if step < NS_ITERS - 1:
                root = system_ref[i]
                system_ref[i] = root + dot(root.astype(BF16), change[i])

    first = pl.multiple_of(rank * PITCH, 8)
    last = pl.multiple_of(ranks * PITCH + rank // 2 * (2 * rest), 8)
    odd = lax.rem(rank, 2) == 1
    ones = jnp.ones((1, ensemble), F32)
    inverses = [split(inverse_ref[i]) for i in range(LIVE)]
    half_way = [
        dot3(split(jnp.broadcast_to(pull[i], (8, side))), inverses[i]) for i in range(LIVE)
    ]
    mean_weights = [dot3(split(half_way[i]), inverses[i])[0:1, :] for i in range(LIVE)]
    for i in range(LIVE):
        mean_weight = mean_weights[i] * (1.0 / frobenius[i])
        ends = inverse_ref[i, pl.ds(last, 2 * rest), :]
        ends = jnp.where(odd, ends[rest:], ends[:rest])
        own = jnp.concatenate([inverse_ref[i, pl.ds(first, PITCH), :], ends], axis=0)
        transform = (math.sqrt(ensemble - 1) * lax.rsqrt(frobenius[i])) * own + mean_weight
        transform = transform[:, :ensemble]
        transform = transform.astype(BF16).astype(F32)
        keep_share = 1.0 - jnp.sum(transform, axis=1, keepdims=True)
        weights = padded_to(jnp.concatenate([transform, ones], axis=0), 2 * PITCH).astype(BF16)
        state = [x for c in range(0, pieces, 2) for x in all_members((tiles + i * pieces + c) // 2)]
        for c in range(pieces):
            blended = dot(weights, state[c])
            mean_state = blended[members : members + 1, :] / ensemble
            analysis = blended[:members] + keep_share * mean_state
            rows_ref[c, pl.ds(i, members, stride=PITCH), :] = jnp.where(i < live_count, analysis, 0.0)
    for i in range(LIVE, capacity):
        for c in range(pieces):
            rows_ref[c, pl.ds(i, members, stride=PITCH), :] = jnp.zeros((members, obs_slots), F32)
    for m in range(members):
        for c in range(pieces):
            span = slice(c * obs_slots, (c + 1) * obs_slots)
            out_ref[m, :, span] = rows_ref[c, m * PITCH : m * PITCH + capacity, :].astype(BF16)


def shards(
    background, obs_ens, innovation, precision, loc_weight,
    old_split, new_split, obs_count, halo_tiles, region_list,
):
    capacity, members, width = background.shape
    obs_slots = obs_ens.shape[2]
    devices = lax.axis_size("tile")
    ranks = lax.axis_size("mem")
    pieces = width // obs_slots
    tiles = LIVE + HPEER * HCAP
    smem = pl.BlockSpec(memory_space=SMEM)
    vmem = pl.BlockSpec(memory_space=VMEM)
    hbm = pl.BlockSpec(memory_space=pltpu.HBM)

    def params(mebibytes):
        return pltpu.CompilerParams(vmem_limit_bytes=mebibytes << 20)

    def tile_blocks(*leading):
        return jax.ShapeDtypeStruct((*leading, PADDED, obs_slots), BF16)

    background, obs_ens = background.transpose(1, 0, 2), obs_ens.transpose(1, 0, 2)
    halo_tiles, region_list, loc_weight = halo_tiles.T, region_list.T, loc_weight.T

    own, own_pulled, block, *swaps = pl.pallas_call(
        pack_kernel,
        out_shape=(
            tile_blocks(LIVE),
            jax.ShapeDtypeStruct((PITCH, obs_slots), F32),
            tile_blocks(BLOCK, HCAP + MOVE * pieces),
            tile_blocks(HCAP),
            tile_blocks(HCAP),
            tile_blocks(HCAP + MOVE * pieces),
        ),
        in_specs=[smem] * 4 + [vmem] * 4,
        out_specs=[vmem] * 6,
        scratch_shapes=[
            VMEM((members * PITCH, obs_slots), F32),
            VMEM((pieces, members * PITCH, obs_slots), F32),
        ],
        compiler_params=params(56),
    )(obs_count, old_split, new_split, halo_tiles, obs_ens, innovation, precision, background)

    groups = [list(range(b, b + BLOCK)) for b in range(0, devices, BLOCK)]
    block = lax.all_to_all(block, "tile", 0, 0, axis_index_groups=groups, tiled=True)
    arrived = []
    for swap, value in zip(SWAPS, swaps):
        pairs = [(d, d + swap[d % BLOCK]) for d in range(devices)]
        pairs = [(d, e) for d, e in pairs if 0 <= e < devices]
        arrived.append(lax.ppermute(value, "tile", pairs))

    table_shape = ((tiles + LIVE * pieces) // 2, 2 * members, obs_slots)
    stays = pl.pallas_call(
        own_table_kernel,
        out_shape=jax.ShapeDtypeStruct((ROOM, *table_shape), BF16),
        in_specs=[smem] * 2 + [vmem] * 2,
        out_specs=pl.BlockSpec(memory_space=pl.ANY),
        scratch_shapes=[
            VMEM(table_shape, BF16),
            VMEM((pieces, members * PITCH, obs_slots), F32),
            pltpu.SemaphoreType.DMA,
        ],
        compiler_params=params(56),
        cost_estimate=COST,
    )(old_split, new_split, own, background)
    table, halo_pulled = pl.pallas_call(
        table_kernel,
        out_shape=(
            jax.ShapeDtypeStruct((ranks, *table_shape), BF16),
            jax.ShapeDtypeStruct((PITCH, obs_slots), F32),
        ),
        in_specs=[smem] * 3 + [pl.BlockSpec(memory_space=pl.ANY)] + [vmem] * 4,
        out_specs=(pl.BlockSpec(memory_space=pl.ANY), vmem),
        scratch_shapes=[
            VMEM(table_shape, BF16),
            pltpu.SemaphoreType.DMA,
            pltpu.SemaphoreType.DMA((ranks,)),
        ],
        compiler_params=params(50),
    )(old_split, new_split, halo_tiles, stays, block, *arrived)
    table = lax.all_to_all(table, "mem", 0, 0, tiled=True)

    side = ranks * members + PITCH
    analysis = pl.pallas_call(
        analysis_kernel,
        out_shape=jax.ShapeDtypeStruct((members, capacity, width), BF16),
        in_specs=[smem] * 3 + [vmem] * 3,
        out_specs=vmem,
        scratch_shapes=[
            VMEM((tiles, side, side), F32),
            VMEM((LIVE, side, side), F32),
            VMEM((LIVE, side, side), F32),
            VMEM((pieces, members * PITCH, obs_slots), F32),
        ],
        compiler_params=params(28),
    )(region_list, loc_weight, new_split, own_pulled, halo_pulled, table)
    return analysis.transpose(1, 0, 2)


def solution(mesh):
    in_specs = (
        P("tile", "mem", None),
        P("tile", "mem", None),
        P("tile", None),
        P("tile", None),
        P("tile", None),
        P(),
        P(),
        P("tile"),
        P(),
        P("tile", None),
    )
    out_specs = P("tile", "mem", None)
    return jax.shard_map(shards, mesh=mesh, in_specs=in_specs, out_specs=out_specs, check_vma=False)
```
